32 devices in a mesh: region: 8 (over y, x, core), sub: 4 (over z).
Axes of the slice: x: 2, y: 2, z: 4, core: 2. Of those that a mesh axis runs over, the one named last changes fastest.
Arguments:
- state_anom: bfloat16 [64, 64, 4096], P(('region', 'sub')), may hold values from -6 to 6
- obs_anom: bfloat16 [768, 64, 128], P(('region', 'sub')), may hold values from -6 to 6
- innovations: bfloat16 [768, 128], P(('region', 'sub')), may hold values from -6 to 6
- obs_error: bfloat16 [768, 128], P(('region', 'sub')), may hold values from 2 to 16
- influence: int32 [768, 4], P(('region', 'sub')), may hold values from 0 to 63, as said below
- taper_level: int32 [768, 4], P(('region', 'sub')), may hold values from 0 to 3
- obs_count: int32 [8], P('region'), may hold values from 3072 to 12288
Outputs:
- increment: float32 [64, 4096], P(('region', 'sub'))
- variance_drop: float32 [64, 4096], P(('region', 'sub'))
The draws below stay inside these ranges and needn't reach their ends.
Inputs may be any that keep to these rules, and one draw needn't show every extreme that they name: `influence`: every listed column block lies in the observation block's own region or in a region one index away (regions wrap around). Over the blocks of one device, at most 36 entries name column blocks held by devices of one sub index, and exactly 36 for some sub index.
All inputs are finite; a program needn't handle non-finite values.
Results may differ from the reference program's by a relative error of at most 0.013.
Values may be sent and summed in bfloat16 or wider, within the bound.
No kernel may reach another device: no remote copies, remote signals or barrier semaphores. Data moves between devices by JAX's collectives and lax.ppermute only.
A program may use at most 64 MiB of HBM per device.

```python
import math
import jax
import jax.numpy as jnp
from jax import lax

M = 64
OB = 128
NINF = 4
OBLK_DEV = 24
CBLK_DEV = 2
CB = 4096
REGIONS = 8
SUBS = 4
CAP = 36
OBS_REG = 12288
OBS_BLOCKS = 768
COL_BLOCKS = 64


def draw_influence(key, part):
    key = jax.random.fold_in(key, 11)
    pairs = OBLK_DEV * NINF
    pool_size = SUBS * CAP

    def one_device(device):
        dev_key = jax.random.fold_in(key, device)
        keys = jax.random.split(dev_key, 5)
        pool = jnp.repeat(jnp.arange(SUBS, dtype=jnp.int32), CAP)
        leader = jax.random.randint(keys[0], (), 0, SUBS, dtype=jnp.int32)
        scores = jax.random.permutation(keys[1], pool_size).astype(jnp.int32)
        scores = jnp.where(pool == leader, -1, scores)
        order = jnp.argsort(scores, stable=True)
        chosen = pool[order][:pairs]
        chosen = chosen[jax.random.permutation(keys[2], pairs)]
        raw_offset = jax.random.randint(keys[3], (pairs,), 0, 4, dtype=jnp.int32)
        offset = jnp.where(raw_offset == 0, -1, jnp.where(raw_offset == 3, 1, 0))
        local = jax.random.randint(keys[4], (pairs,), 0, CBLK_DEV, dtype=jnp.int32)
        region_id = device // SUBS
        target_region = (region_id + offset + REGIONS) % REGIONS
        target = target_region * SUBS * CBLK_DEV + chosen * CBLK_DEV + local
        return target.reshape(OBLK_DEV, NINF)
    result = jax.vmap(one_device)(jnp.arange(REGIONS * SUBS, dtype=jnp.int32))
    return result.reshape(OBS_BLOCKS, NINF).astype(jnp.int32)


def draw_obs_count(key, part):
    key = jax.random.fold_in(key, 5)
    keys = jax.random.split(key, 2)
    lowest = OBS_REG // 4
    counts = jax.random.randint(keys[0], (REGIONS,), lowest, OBS_REG + 1, dtype=jnp.int32)
    order = jax.random.permutation(keys[1], REGIONS)
    counts = counts.at[order[0]].set(OBS_REG)
    counts = counts.at[order[1]].set(lowest)
    return counts.astype(jnp.int32)


def set_ends(entries, stream_key, low, largest):
    longest = entries.shape.index(max(entries.shape))
    spots = []
    for shift in (0, 1):
        where = [jax.random.randint(jax.random.fold_in(stream_key, axis), (), 0, length) for axis, length in enumerate(entries.shape)]
        where[longest] = (where[longest] + shift) % entries.shape[longest]
        spots.append(tuple(where))
    return entries.at[spots[0]].set(low).at[spots[1]].set(largest)


def block_scale(stream_key, extent, shards, least, top_value):
    level = 1.0
    for axis_at, blocks in shards:
        heights = jax.random.uniform(jax.random.fold_in(jax.random.fold_in(stream_key, 6), axis_at), (blocks,), jnp.float32, least / len(shards), top_value / len(shards))
        level = level * jnp.repeat(jnp.exp(heights), extent[axis_at] // blocks).reshape((-1,) + (1,) * (len(extent) - 1 - axis_at))
    return level


def noise(key, dims, scale, reach, cuts=(), kind=jnp.bfloat16):
    level = block_scale(key, dims, cuts, -0.22, 0.18) if cuts else 1.0
    array = jax.random.normal(key, dims, jnp.float32) * scale * level
    return jnp.minimum(jnp.maximum(array, -reach), reach).astype(kind)


def setup_inputs(seed: int = 0) -> dict:
    streams_of = jax.random.split(jax.random.key(seed), 8)
    return {
        "state_anom": noise(streams_of[0], (COL_BLOCKS, M, CB), 1.0, 6.0, ((0, 32),)),
        "obs_anom": noise(streams_of[1], (OBS_BLOCKS, M, OB), 1.0, 6.0, ((0, 32),)),
        "innovations": noise(streams_of[2], (OBS_BLOCKS, OB), 1.0, 6.0, ((0, 32),)),
        "obs_error": jnp.clip(jnp.exp(math.log(16.0) - 2.0794415 * jax.random.uniform(streams_of[3], (OBS_BLOCKS, OB), jnp.float32) ** block_scale(streams_of[3], (OBS_BLOCKS, OB), ((0, 32),), -0.2, 0.2)), 2.0, 16.0).astype(jnp.bfloat16),
        "influence": draw_influence(jax.random.fold_in(streams_of[7], 71), 0),
        "taper_level": set_ends(jax.random.randint(streams_of[5], (OBS_BLOCKS, NINF), 0, 4), jax.random.fold_in(streams_of[5], 1), 0, 3).astype(jnp.int32),
        "obs_count": draw_obs_count(jax.random.fold_in(streams_of[7], 71), 0),
    }


def block_terms(obs_blocks, innov_blocks, error_blocks, first_block, obs_total):
    blocks = obs_blocks.shape[0]
    divisor = M - 1.0
    values = obs_blocks.astype(jnp.float32)
    spread = jnp.sum(values * values, axis=1) / divisor
    position = (first_block + jnp.arange(blocks, dtype=jnp.int32))[:, None] * OB + jnp.arange(OB, dtype=jnp.int32)[None, :]
    usable = (position < obs_total).astype(jnp.float32)
    factor = usable / (spread + error_blocks.astype(jnp.float32))
    scaled = (values * (factor / (divisor * divisor))[:, None, :]).astype(jnp.bfloat16)
    scaled_f = scaled.astype(jnp.float32)
    covariance = jnp.einsum('bmo,bno->bmn', scaled_f, values)
    weights = divisor * jnp.einsum('bmo,bo->bm', scaled_f, innov_blocks.astype(jnp.float32))
    return jnp.concatenate([weights, covariance.reshape(blocks, M * M)], axis=1)


def reference(state_anom, obs_anom, innovations, obs_error, influence, taper_level, obs_count):
    per_region = OBLK_DEV * SUBS
    col_total = state_anom.shape[0]
    totals = jnp.zeros((col_total, M * M + M), jnp.float32)

    def region_step(totals, region_id):
        first = region_id * per_region
        obs_blocks = lax.dynamic_slice_in_dim(obs_anom, first, per_region, 0)
        innov_blocks = lax.dynamic_slice_in_dim(innovations, first, per_region, 0)
        error_blocks = lax.dynamic_slice_in_dim(obs_error, first, per_region, 0)
        targets = lax.dynamic_slice_in_dim(influence, first, per_region, 0)
        levels = lax.dynamic_slice_in_dim(taper_level, first, per_region, 0)
        partials = block_terms(obs_blocks, innov_blocks, error_blocks, jnp.int32(0), obs_count[region_id])
        tapers = 1.0 - 0.25 * levels.astype(jnp.float32)
        pieces = (tapers[:, :, None] * partials[:, None, :]).reshape(per_region * NINF, M * M + M)
        totals = totals.at[targets.reshape(-1)].add(pieces)
        return totals, None

    totals, unused = lax.scan(region_step, totals, jnp.arange(REGIONS, dtype=jnp.int32))
    mixer = jnp.concatenate([totals[:, None, :M], totals[:, M:].reshape(col_total, M, M)], axis=1).astype(jnp.bfloat16)

    def column_block(pair):
        mix_block, state_block = pair
        projected = jnp.dot(mix_block, state_block, preferred_element_type=jnp.float32)
        drop = jnp.sum(state_block.astype(jnp.float32) * projected[1:], axis=0)
        return projected[0], drop

    increment, variance_drop = lax.map(column_block, (mixer, state_anom))
    return increment, variance_drop
```

```python
import functools

import jax
import jax.numpy as jnp
from jax import lax
from jax.experimental import pallas as pl
from jax.experimental.pallas import tpu as pltpu
from jax.sharding import PartitionSpec as P

AXES = ("region", "sub")
HALF = 32
SLOT = 48
USED = 40


def lane_patterns(rows):
    row = lax.broadcasted_iota(jnp.int32, (rows, 128), 0)
    lane = lax.broadcasted_iota(jnp.int32, (rows, 128), 1)
    return row, lane, lane % HALF, (lane // HALF) % 2 == 0


def pack_weights(infl_ref, level_ref, rows_ref, weights_ref, group_regions, sub_here, sub_count):
    blocks = infl_ref.shape[1]
    rows_ref[...] = jnp.zeros_like(rows_ref)
    rows_ref[0:4, 0:blocks] = infl_ref[...].astype(jnp.float32)
    rows_ref[4:8, 0:blocks] = 1.0 - 0.25 * level_ref[...].astype(jnp.float32)
    columns = rows_ref[...].T
    targets = [jnp.broadcast_to(columns[0:blocks, n : n + 1], (blocks, 128)) for n in range(4)]
    tapers = [jnp.broadcast_to(columns[0:blocks, 4 + n : 5 + n], (blocks, 128)) for n in range(4)]
    local = lax.broadcasted_iota(jnp.int32, (blocks, 128), 1) // 64
    for g, region in enumerate(group_regions):
        for k, slot in enumerate(slot_order(sub_count)):
            first = (region * sub_count + (sub_here ^ slot)) * 2
            wanted = (first + local).astype(jnp.float32)
            weight = jnp.zeros((blocks, 128), jnp.float32)
            for n in range(4):
                weight = weight + jnp.where(targets[n] == wanted, tapers[n], 0.0)
            weights_ref[g * sub_count + k] = weight


def slot_order(sub_count):
    bits = sub_count.bit_length() - 1
    return sorted(range(sub_count), key=lambda i: [(i >> b) & 1 for b in range(bits)])


def neighbours(regions):
    here = lax.axis_index("region")
    odd = here % 2
    far = (here + 2 * odd - 1 + regions) % regions
    near = here + 1 - 2 * odd
    return here, near, far


def terms_kernel(sub_count, regions, count_ref, infl_ref, level_ref, obs_ref, innov_ref, error_ref,
                 terms_ref, weights_ref, far_ref, rows_ref, error32, innov32):
    blocks, members, per_block = obs_ref.shape
    here, near, far = neighbours(regions)
    sub_here = lax.axis_index("sub")
    divisor = members - 1.0
    error32[...] = error_ref[...].astype(jnp.float32)
    innov32[...] = innov_ref[...].astype(jnp.float32)
    pack_weights(infl_ref, level_ref, rows_ref, weights_ref, (far, near, here), sub_here, sub_count)
    row, lane, column, square = lane_patterns(HALF)
    upper = (row <= column) | ~square
    diagonal = (row == column) & square
    row8 = lax.broadcasted_iota(jnp.int32, (8, 128), 0)
    place = lax.broadcasted_iota(jnp.int32, (1, 128), 1)
    left = count_ref[0] - sub_here * (blocks * per_block)
    for b in range(blocks):
        raw = obs_ref[b]
        values = raw.astype(jnp.float32)
        spread = jnp.sum(values * values, axis=0, keepdims=True) / divisor
        usable = jnp.where(place + b * per_block < left, 1.0 / (divisor * divisor), 0.0)
        factor = usable / (spread + error32[b : b + 1, :])
        scaled = (values * factor).astype(jnp.bfloat16)
        low, high = scaled[:HALF], scaled[HALF:]
        innov = jnp.broadcast_to(innov32[b : b + 1, :], (16, 128)).astype(jnp.bfloat16)
        product = lax.dot_general(
            jnp.concatenate([raw, innov], axis=0),
            jnp.concatenate([low, high, low, high, high, low, high, low], axis=0),
            (((1,), (1,)), ((), ())),
            preferred_element_type=jnp.float32,
        )
        lower = product[HALF : 2 * HALF, 128:]
        terms_ref[b, 0:HALF, :] = jnp.where(upper, product[:HALF, :128], lower)
        corner = jnp.sum(jnp.where(diagonal, lower, 0.0), axis=0, keepdims=True)
        extra = jnp.where(row8 == 0, divisor * product[2 * HALF : 2 * HALF + 8, :128], jnp.where(row8 == 1, corner, 0.0))
        terms_ref[b, HALF:USED, :] = extra
    write_sums(weights_ref, terms_ref, 0, sub_count, far_ref)


def write_sums(weights_ref, terms_ref, first, sub_count, out_ref):
    blocks = terms_ref.shape[0]
    for k in range(0, sub_count, 4):
        count = min(4, sub_count - k)
        totals = [jnp.zeros((USED, 128), jnp.float32) for _ in range(count)]
        for b in range(blocks):
            term = terms_ref[b]
            for i in range(count):
                totals[i] = totals[i] + weights_ref[first + k + i, b : b + 1, :] * term
        for i in range(count):
            whole = jnp.concatenate([totals[i], jnp.zeros((SLOT - USED, 128), jnp.float32)], axis=0)
            out_ref[(k + i) * SLOT : (k + i + 1) * SLOT, :] = whole.astype(out_ref.dtype)


def rest_kernel(sub_count, terms_ref, weights_ref, near_ref, here_ref):
    write_sums(weights_ref, terms_ref, sub_count, sub_count, near_ref)
    write_sums(weights_ref, terms_ref, 2 * sub_count, sub_count, here_ref)


def project_kernel(kept_ref, got_ref, state_ref, increment_ref, drop_ref):
    total = kept_ref[...] + got_ref[...].astype(jnp.float32)
    row, lane, column, square = lane_patterns(HALF)
    packed = total[:HALF]
    shifted = pltpu.roll(packed, HALF, 1)
    corner = pltpu.roll(jnp.broadcast_to(total[HALF + 1 : HALF + 2], (HALF, 128)), HALF, 1)
    first = lane < 64
    top = packed * jnp.where(square, jnp.where(row < column, 2.0, jnp.where(row == column, 1.0, 0.0)), 2.0)
    bottom = jnp.where(square, 0.0, jnp.where(row > column, 2.0 * shifted, jnp.where(row == column, corner, 0.0)))
    row16, lane16, _, _ = lane_patterns(16)
    weights = jnp.broadcast_to(total[HALF : HALF + 1], (16, 128))
    weights = jnp.where(row16 == lane16 // 64, weights, 0.0)
    mixer = jnp.concatenate(
        [
            jnp.where(first, top, 0.0),
            jnp.where(first, bottom, 0.0),
            jnp.where(first, 0.0, top),
            jnp.where(first, 0.0, bottom),
            weights,
        ],
        axis=0,
    ).astype(jnp.bfloat16)
    width = 512
    for at in range(0, state_ref.shape[1], width):
        state = state_ref[:, at : at + width]
        projected = jnp.dot(mixer, state, preferred_element_type=jnp.float32)
        product = state.astype(jnp.float32) * projected[:128]
        increment_ref[:, at : at + width] = projected[128:130]
        drop_ref[0:1, at : at + width] = jnp.sum(product[:64], axis=0, keepdims=True)
        drop_ref[1:2, at : at + width] = jnp.sum(product[64:], axis=0, keepdims=True)


def local(state_anom, obs_anom, innovations, obs_error, influence, taper_level, obs_count):
    sub_count = lax.axis_size("sub")
    regions = lax.axis_size("region")
    col_blocks, members, cells = state_anom.shape
    blocks = obs_anom.shape[0]
    assert (col_blocks, members, obs_anom.shape[2]) == (2, 64, 128)
    assert regions % 2 == 0 and sub_count & (sub_count - 1) == 0
    vmem = pl.BlockSpec(memory_space=pltpu.VMEM)
    smem = pl.BlockSpec(memory_space=pltpu.SMEM)
    rows = sub_count * SLOT
    terms, weights, far = pl.pallas_call(
        functools.partial(terms_kernel, sub_count, regions),
        out_shape=(
            jax.ShapeDtypeStruct((blocks, USED, 128), jnp.float32),
            jax.ShapeDtypeStruct((3 * sub_count, blocks, 128), jnp.float32),
            jax.ShapeDtypeStruct((rows, 128), jnp.bfloat16),
        ),
        in_specs=[smem] + [vmem] * 5,
        out_specs=(vmem, vmem, vmem),
        scratch_shapes=[pltpu.VMEM((8, 128), jnp.float32)] + [pltpu.VMEM((blocks, 128), jnp.float32)] * 2,
        cost_estimate=pl.CostEstimate(flops=2 * blocks * 80 * 256 * 128, bytes_accessed=blocks * 64 * 128 * 2, transcendentals=0),
    )(obs_count, influence.T, taper_level.T, obs_anom, innovations, obs_error)
    from_far = lax.ppermute(far, "region", [(r, (r + 2 * (r % 2) - 1) % regions) for r in range(regions)])
    near, here = pl.pallas_call(
        functools.partial(rest_kernel, sub_count),
        out_shape=(
            jax.ShapeDtypeStruct((rows, 128), jnp.bfloat16),
            jax.ShapeDtypeStruct((rows, 128), jnp.float32),
        ),
        in_specs=[vmem] * 2,
        out_specs=(vmem, vmem),
        cost_estimate=pl.CostEstimate(flops=4 * blocks * rows * 128, bytes_accessed=blocks * USED * 512, transcendentals=0),
    )(terms, weights)
    from_near = lax.ppermute(near, "region", [(r, r ^ 1) for r in range(regions)])
    total = here + from_near.astype(jnp.float32) + from_far.astype(jnp.float32)
    step = 1
    while step < sub_count:
        half = total.shape[0] // 2
        got = lax.ppermute(total[half:].astype(jnp.bfloat16), "sub", [(s, s ^ step) for s in range(sub_count)])
        kept = total[:half]
        step *= 2
        if step < sub_count:
            total = kept + got.astype(jnp.float32)
    increment, variance_drop = pl.pallas_call(
        project_kernel,
        out_shape=(jax.ShapeDtypeStruct((2, cells), jnp.float32),) * 2,
        in_specs=[vmem] * 3,
        out_specs=(vmem, vmem),
        cost_estimate=pl.CostEstimate(flops=2 * 144 * 128 * cells, bytes_accessed=col_blocks * 64 * cells * 2, transcendentals=0),
    )(kept, got, state_anom.reshape(col_blocks * members, cells))
    return (increment, variance_drop)


def solution(mesh):
    return jax.shard_map(
        local,
        mesh=mesh,
        in_specs=(
            P(AXES, None, None),
            P(AXES, None, None),
            P(AXES, None),
            P(AXES, None),
            P(AXES, None),
            P(AXES, None),
            P("region"),
        ),
        out_specs=(P(AXES, None), P(AXES, None)),
        check_vma=False,
    )
```

```python
import functools

import jax
import jax.numpy as jnp
from jax import lax
from jax.experimental import pallas as pl
from jax.experimental.pallas import tpu as pltpu
from jax.sharding import PartitionSpec as P

AXES = ("region", "sub")
HALF = 32
SLOT = 48
USED = 40
VMEM_LIMIT = 8 * 1024 * 1024


def lane_patterns(rows):
    row = lax.broadcasted_iota(jnp.int32, (rows, 128), 0)
    lane = lax.broadcasted_iota(jnp.int32, (rows, 128), 1)
    return row, lane, lane % HALF, (lane // HALF) % 2 == 0


def pack_weights(infl_ref, level_ref, rows_ref, weights_ref, group_regions, sub_here, sub_count):
    blocks = infl_ref.shape[1]
    rows_ref[...] = jnp.zeros_like(rows_ref)
    rows_ref[0:4, 0:blocks] = infl_ref[...].astype(jnp.float32)
    rows_ref[4:8, 0:blocks] = 1.0 - 0.25 * level_ref[...].astype(jnp.float32)
    columns = rows_ref[...].T
    targets = [jnp.broadcast_to(columns[0:blocks, n : n + 1], (blocks, 128)) for n in range(4)]
    tapers = [jnp.broadcast_to(columns[0:blocks, 4 + n : 5 + n], (blocks, 128)) for n in range(4)]
    local = lax.broadcasted_iota(jnp.int32, (blocks, 128), 1) // 64
    for g, region in enumerate(group_regions):
        for k, slot in enumerate(slot_order(sub_count)):
            first = (region * sub_count + (sub_here ^ slot)) * 2
            wanted = (first + local).astype(jnp.float32)
            weight = jnp.zeros((blocks, 128), jnp.float32)
            for n in range(4):
                weight = weight + jnp.where(targets[n] == wanted, tapers[n], 0.0)
            weights_ref[g * sub_count + k] = weight


def slot_order(sub_count):
    bits = sub_count.bit_length() - 1
    return sorted(range(sub_count), key=lambda i: [(i >> b) & 1 for b in range(bits)])


def neighbours(regions):
    here = lax.axis_index("region")
    odd = here % 2
    far = (here + 2 * odd - 1 + regions) % regions
    near = here + 1 - 2 * odd
    return here, near, far


def terms_kernel(sub_count, regions, count_ref, infl_hbm, level_hbm, innov_hbm, error_hbm, obs_hbm,
                 terms_ref, weights_ref, far_ref,
                 infl_ref, level_ref, innov_ref, error_ref, obs_ref, rows_ref, error32, innov32, small_sems, obs_sem):
    blocks, members, per_block = obs_ref.shape
    pairs = ((infl_hbm, infl_ref), (level_hbm, level_ref), (innov_hbm, innov_ref), (error_hbm, error_ref))
    small = [pltpu.make_async_copy(pair[0], pair[1], small_sems.at[i]) for i, pair in enumerate(pairs)]
    for copy in small:
        copy.start()
    large = pltpu.make_async_copy(obs_hbm, obs_ref, obs_sem)
    large.start()
    for copy in small:
        copy.wait()
    here, near, far = neighbours(regions)
    sub_here = lax.axis_index("sub")
    divisor = members - 1.0
    error32[...] = error_ref[...].astype(jnp.float32)
    innov32[...] = innov_ref[...].astype(jnp.float32)
    pack_weights(infl_ref, level_ref, rows_ref, weights_ref, (far, near, here), sub_here, sub_count)
    row, lane, column, square = lane_patterns(HALF)
    upper = (row <= column) | ~square
    diagonal = (row == column) & square
    row8 = lax.broadcasted_iota(jnp.int32, (8, 128), 0)
    place = lax.broadcasted_iota(jnp.int32, (1, 128), 1)
    left = count_ref[0] - sub_here * (blocks * per_block)
    large.wait()
    for b in range(blocks):
        raw = obs_ref[b]
        values = raw.astype(jnp.float32)
        spread = jnp.sum(values * values, axis=0, keepdims=True) / divisor
        usable = jnp.where(place + b * per_block < left, 1.0 / (divisor * divisor), 0.0)
        factor = usable / (spread + error32[b : b + 1, :])
        scaled = (values * factor).astype(jnp.bfloat16)
        low, high = scaled[:HALF], scaled[HALF:]
        innov = jnp.broadcast_to(innov32[b : b + 1, :], (16, 128)).astype(jnp.bfloat16)
        product = lax.dot_general(
            jnp.concatenate([raw, innov], axis=0),
            jnp.concatenate([low, high, low, high, high, low, high, low], axis=0),
            (((1,), (1,)), ((), ())),
            preferred_element_type=jnp.float32,
        )
        lower = product[HALF : 2 * HALF, 128:]
        terms_ref[b, 0:HALF, :] = jnp.where(upper, product[:HALF, :128], lower)
        corner = jnp.sum(jnp.where(diagonal, lower, 0.0), axis=0, keepdims=True)
        extra = jnp.where(row8 == 0, divisor * product[2 * HALF : 2 * HALF + 8, :128], jnp.where(row8 == 1, corner, 0.0))
        terms_ref[b, HALF:USED, :] = extra
    write_sums(weights_ref, terms_ref, 0, sub_count, far_ref)


def write_sums(weights_ref, terms_ref, first, sub_count, out_ref):
    blocks = terms_ref.shape[0]
    stride = out_ref.shape[0] // sub_count
    rest = [jnp.zeros((stride - USED, 128), jnp.float32)] if stride > USED else []
    group = min(4, sub_count)
    for k in range(0, sub_count, group):
        totals = [jnp.zeros((USED, 128), jnp.float32) for _ in range(group)]
        for b in range(blocks):
            term = terms_ref[b]
            for i in range(group):
                totals[i] = totals[i] + weights_ref[first + k + i, b : b + 1, :] * term
        whole = jnp.concatenate([part for total in totals for part in [total] + rest], axis=0)
        out_ref[k * stride : (k + group) * stride, :] = whole.astype(out_ref.dtype)


def rest_kernel(sub_count, terms_ref, weights_ref, near_ref, here_ref):
    write_sums(weights_ref, terms_ref, sub_count, sub_count, near_ref)
    write_sums(weights_ref, terms_ref, 2 * sub_count, sub_count, here_ref)


def project_kernel(total_ref, state_ref, increment_ref, drop_ref):
    total = total_ref[...]
    row, lane, column, square = lane_patterns(HALF)
    packed = total[:HALF]
    shifted = pltpu.roll(packed, HALF, 1)
    corner = pltpu.roll(jnp.broadcast_to(total[HALF + 1 : HALF + 2], (HALF, 128)), HALF, 1)
    first = lane < 64
    top = packed * jnp.where(square, jnp.where(row < column, 2.0, jnp.where(row == column, 1.0, 0.0)), 2.0)
    bottom = jnp.where(square, 0.0, jnp.where(row > column, 2.0 * shifted, jnp.where(row == column, corner, 0.0)))
    row16, lane16, _, _ = lane_patterns(16)
    weights = jnp.broadcast_to(total[HALF : HALF + 1], (16, 128))
    weights = jnp.where(row16 == lane16 // 64, weights, 0.0)
    mixer = jnp.concatenate(
        [
            jnp.where(first, top, 0.0),
            jnp.where(first, bottom, 0.0),
            jnp.where(first, 0.0, top),
            jnp.where(first, 0.0, bottom),
            weights,
        ],
        axis=0,
    ).astype(jnp.bfloat16)
    width = 512
    for at in range(0, state_ref.shape[1], width):
        state = state_ref[:, at : at + width]
        projected = jnp.dot(mixer, state, preferred_element_type=jnp.float32)
        product = state.astype(jnp.float32) * projected[:128]
        increment_ref[:, at : at + width] = projected[128:130]
        drop_ref[0:1, at : at + width] = jnp.sum(product[:64], axis=0, keepdims=True)
        drop_ref[1:2, at : at + width] = jnp.sum(product[64:], axis=0, keepdims=True)


def narrow(sums, count):
    return sums.reshape(count, -1, 128)[:, :USED].astype(jnp.float32)


def local(state_anom, obs_anom, innovations, obs_error, influence, taper_level, obs_count):
    sub_count = lax.axis_size("sub")
    regions = lax.axis_size("region")
    col_blocks, members, cells = state_anom.shape
    blocks = obs_anom.shape[0]
    assert (col_blocks, members, obs_anom.shape[2]) == (2, 64, 128)
    assert regions % 2 == 0 and sub_count in (4, 16, 64)
    vmem = pl.BlockSpec(memory_space=pltpu.VMEM)
    rows = sub_count * SLOT
    terms, weights, far = pl.pallas_call(
        functools.partial(terms_kernel, sub_count, regions),
        out_shape=(
            jax.ShapeDtypeStruct((blocks, USED, 128), jnp.float32),
            jax.ShapeDtypeStruct((3 * sub_count, blocks, 128), jnp.float32),
            jax.ShapeDtypeStruct((rows, 128), jnp.bfloat16),
        ),
        in_specs=[pl.BlockSpec(memory_space=pltpu.SMEM)] + [pl.BlockSpec(memory_space=pltpu.HBM)] * 5,
        out_specs=(vmem, vmem, vmem),
        scratch_shapes=[
            pltpu.VMEM((4, blocks), jnp.int32),
            pltpu.VMEM((4, blocks), jnp.int32),
            pltpu.VMEM(innovations.shape, jnp.bfloat16),
            pltpu.VMEM(obs_error.shape, jnp.bfloat16),
            pltpu.VMEM(obs_anom.shape, jnp.bfloat16),
            pltpu.VMEM((8, 128), jnp.float32),
            pltpu.VMEM((blocks, 128), jnp.float32),
            pltpu.VMEM((blocks, 128), jnp.float32),
            pltpu.SemaphoreType.DMA((4,)),
            pltpu.SemaphoreType.DMA,
        ],
        compiler_params=pltpu.CompilerParams(vmem_limit_bytes=VMEM_LIMIT),
        cost_estimate=pl.CostEstimate(flops=2 * blocks * 80 * 256 * 128, bytes_accessed=blocks * 64 * 128 * 2, transcendentals=0),
    )(obs_count, *[pltpu.with_memory_space_constraint(x, pltpu.HBM) for x in (influence.T, taper_level.T, innovations, obs_error, obs_anom)])
    state_anom, far = lax.optimization_barrier((state_anom, far))
    from_far = lax.ppermute(far, "region", [(r, (r + 2 * (r % 2) - 1) % regions) for r in range(regions)])
    near, here = pl.pallas_call(
        functools.partial(rest_kernel, sub_count),
        out_shape=(
            jax.ShapeDtypeStruct((sub_count * USED, 128), jnp.bfloat16),
            jax.ShapeDtypeStruct((sub_count * USED, 128), jnp.float32),
        ),
        in_specs=[vmem] * 2,
        out_specs=(vmem, vmem),
        compiler_params=pltpu.CompilerParams(vmem_limit_bytes=VMEM_LIMIT),
        cost_estimate=pl.CostEstimate(flops=4 * blocks * rows * 128, bytes_accessed=blocks * USED * 512, transcendentals=0),
    )(terms, weights)
    devices = [(r, s) for r in range(regions) for s in range(sub_count)]
    place = {device: i for i, device in enumerate(devices)}
    beside = [(place[r, s], place[r ^ 1, s]) for r, s in devices]
    from_near = lax.ppermute(near, AXES, beside)

    total = here.reshape(sub_count, USED, 128) + (narrow(from_far, sub_count) + narrow(from_near, sub_count))
    step = 1
    while step < sub_count:
        half = total.shape[0] // 2
        sent = jnp.pad(total[half:], ((0, 0), (0, SLOT - USED), (0, 0))).reshape(half * SLOT, 128).astype(jnp.bfloat16)
        kept = total[:half].reshape(half * USED, 128).astype(jnp.bfloat16)
        got = lax.ppermute(sent, AXES, [(place[r, s], place[r ^ 1, s ^ step]) for r, s in devices])
        kept = lax.ppermute(kept, AXES, beside)
        total = narrow(kept, half) + narrow(got, half)
        step *= 2
    increment, variance_drop = pl.pallas_call(
        project_kernel,
        out_shape=(jax.ShapeDtypeStruct((2, cells), jnp.float32),) * 2,
        in_specs=[vmem] * 2,
        out_specs=(vmem, vmem),
        compiler_params=pltpu.CompilerParams(vmem_limit_bytes=VMEM_LIMIT),
        cost_estimate=pl.CostEstimate(flops=2 * 144 * 128 * cells, bytes_accessed=col_blocks * 64 * cells * 2, transcendentals=0),
    )(total[0], state_anom.reshape(col_blocks * members, cells))
    return (increment, variance_drop)


def solution(mesh):
    return jax.shard_map(
        local,
        mesh=mesh,
        in_specs=(
            P(AXES, None, None),
            P(AXES, None, None),
            P(AXES, None),
            P(AXES, None),
            P(AXES, None),
            P(AXES, None),
            P("region"),
        ),
        out_specs=(P(AXES, None), P(AXES, None)),
        check_vma=False,
    )
```

```python
import functools

import jax
import jax.numpy as jnp
from jax import lax
from jax.experimental import pallas as pl
from jax.experimental.pallas import tpu as pltpu
from jax.sharding import PartitionSpec as P

AXES = ("region", "sub")
HALF = 32
USED = 40
HEAD_COST = pl.CostEstimate(flops=10**10, bytes_accessed=10**8, transcendentals=0)
VMEM_LIMIT = 8 * 1024 * 1024


def lane_patterns(rows):
    row = lax.broadcasted_iota(jnp.int32, (rows, 128), 0)
    lane = lax.broadcasted_iota(jnp.int32, (rows, 128), 1)
    return row, lane, lane % HALF, (lane // HALF) % 2 == 0


def pack_weights(infl_ref, level_ref, rows_ref, weights_ref, group_regions, sub_here, sub_count):
    blocks = infl_ref.shape[1]
    rows_ref[...] = jnp.zeros_like(rows_ref)
    rows_ref[0:4, 0:blocks] = infl_ref[...].astype(jnp.float32)
    rows_ref[4:8, 0:blocks] = 1.0 - 0.25 * level_ref[...].astype(jnp.float32)
    columns = rows_ref[...].T
    targets = [jnp.broadcast_to(columns[0:blocks, n : n + 1], (blocks, 128)) for n in range(4)]
    tapers = [jnp.broadcast_to(columns[0:blocks, 4 + n : 5 + n], (blocks, 128)) for n in range(4)]
    local = lax.broadcasted_iota(jnp.int32, (blocks, 128), 1) // 64
    for g, region in enumerate(group_regions):
        for k, slot in enumerate(slot_order(sub_count)):
            first = (region * sub_count + (sub_here ^ slot)) * 2
            wanted = (first + local).astype(jnp.float32)
            weight = jnp.zeros((blocks, 128), jnp.float32)
            for n in range(4):
                weight = weight + jnp.where(targets[n] == wanted, tapers[n], 0.0)
            weights_ref[g * sub_count + k] = weight


def slot_order(sub_count):
    bits = sub_count.bit_length() - 1
    return sorted(range(sub_count), key=lambda i: [(i >> b) & 1 for b in range(bits)])


def neighbours(regions):
    here = lax.axis_index("region")
    odd = here % 2
    far = (here + 2 * odd - 1 + regions) % regions
    near = here + 1 - 2 * odd
    return here, near, far


def place_kernel(out_ref):
    out_ref[...] = lax.broadcasted_iota(jnp.int32, (1, 128), 1)


def terms_kernel(sub_count, regions, count_ref, place_ref, infl_ref, level_ref, innov_ref, error_ref, obs_ref,
                 terms_ref, weights_ref, far_ref, rows_ref, error32, innov32):
    blocks, members, per_block = obs_ref.shape
    here, near, far = neighbours(regions)
    sub_here = lax.axis_index("sub")
    divisor = members - 1.0
    error32[...] = error_ref[...].astype(jnp.float32)
    innov32[...] = innov_ref[...].astype(jnp.float32)
    pack_weights(infl_ref, level_ref, rows_ref, weights_ref, (far, near, here), sub_here, sub_count)
    row, lane, column, square = lane_patterns(HALF)
    upper = (row <= column) | ~square
    diagonal = (row == column) & square
    row8 = lax.broadcasted_iota(jnp.int32, (8, 128), 0)
    place = place_ref[...]
    left = count_ref[0] - sub_here * (blocks * per_block)
    for b in range(blocks):
        raw = obs_ref[b]
        values = raw.astype(jnp.float32)
        spread = jnp.sum(values * values, axis=0, keepdims=True) / divisor
        usable = jnp.where(place + b * per_block < left, 1.0 / (divisor * divisor), 0.0)
        factor = usable / (spread + error32[b : b + 1, :])
        scaled = (values * factor).astype(jnp.bfloat16)
        low, high = scaled[:HALF], scaled[HALF:]
        innov = jnp.broadcast_to(innov32[b : b + 1, :], (16, 128)).astype(jnp.bfloat16)
        product = lax.dot_general(
            jnp.concatenate([raw, innov], axis=0),
            jnp.concatenate([low, high, low, high, high, low, high, low], axis=0),
            (((1,), (1,)), ((), ())),
            preferred_element_type=jnp.float32,
        )
        lower = product[HALF : 2 * HALF, 128:]
        terms_ref[b, 0:HALF, :] = jnp.where(upper, product[:HALF, :128], lower)
        corner = jnp.sum(jnp.where(diagonal, lower, 0.0), axis=0, keepdims=True)
        extra = jnp.where(row8 % 2 == 0, divisor * product[2 * HALF : 2 * HALF + 8, :128], corner)
        terms_ref[b, HALF:USED, :] = extra
    write_sums(weights_ref, terms_ref, 0, sub_count, far_ref)


def write_sums(weights_ref, terms_ref, first, sub_count, out_ref):
    blocks = terms_ref.shape[0]
    pair = lax.broadcasted_iota(jnp.int32, (8, 128), 0) // 2
    matrices, extras = [], []
    for k in range(0, sub_count, 4):
        totals = [jnp.zeros((USED, 128), jnp.float32) for _ in range(4)]
        for b in range(blocks):
            term = terms_ref[b]
            for i in range(4):
                totals[i] = totals[i] + weights_ref[first + k + i, b : b + 1, :] * term
        matrices += [total[:HALF] for total in totals]
        extra = totals[3][HALF:]
        for i in range(3):
            extra = jnp.where(pair == i, totals[i][HALF:], extra)
        extras.append(extra)
    rest = out_ref.shape[0] - sub_count * (HALF + 2)
    if rest:
        extras.append(jnp.zeros((rest, 128), jnp.float32))
    out_ref[...] = jnp.concatenate(matrices + extras, axis=0).astype(out_ref.dtype)


def rest_kernel(sub_count, terms_ref, weights_ref, near_ref, here_ref):
    write_sums(weights_ref, terms_ref, sub_count, sub_count, near_ref)
    write_sums(weights_ref, terms_ref, 2 * sub_count, sub_count, here_ref)


def added(count, refs):
    total = sum(ref[...].astype(jnp.float32)[: sum_rows(count, 8)] for ref in refs)
    return total[: count * HALF], total[count * HALF :]


def sum_rows(count, multiple):
    return count * HALF + -(-2 * count // multiple) * multiple


def fold_kernel(count, *refs):
    *sums, sent_ref, kept_ref = refs
    matrix, extra = added(count, sums)
    half = count // 2
    if half % 4:
        high = pltpu.roll(extra, 8 - 2 * half, 0)
        low = extra
    else:
        low, high = extra[: 2 * half], extra[2 * half :]
    fill = sent_ref.shape[0] - sum_rows(half, 8)
    pad = [jnp.zeros((fill, 128), jnp.float32)] if fill else []
    sent_ref[...] = jnp.concatenate([matrix[half * HALF :], high] + pad, axis=0).astype(sent_ref.dtype)
    kept_ref[...] = jnp.concatenate([matrix[: half * HALF], low], axis=0).astype(kept_ref.dtype)


def project_kernel(kept_ref, got_ref, state_ref, increment_ref, drop_ref):
    matrix, extra = added(1, (kept_ref, got_ref))
    row, lane, column, square = lane_patterns(HALF)
    shifted = pltpu.roll(matrix, HALF, 1)
    corner = pltpu.roll(jnp.broadcast_to(extra[1:2], (HALF, 128)), HALF, 1)
    first = lane < 64
    top = matrix * jnp.where(square, jnp.where(row < column, 2.0, jnp.where(row == column, 1.0, 0.0)), 2.0)
    bottom = jnp.where(square, 0.0, jnp.where(row > column, 2.0 * shifted, jnp.where(row == column, corner, 0.0)))
    row16, lane16, _, _ = lane_patterns(16)
    weights = jnp.broadcast_to(extra[0:1], (16, 128))
    weights = jnp.where(row16 == lane16 // 64, weights, 0.0)
    mixer = jnp.concatenate(
        [
            jnp.where(first, top, 0.0),
            jnp.where(first, bottom, 0.0),
            jnp.where(first, 0.0, top),
            jnp.where(first, 0.0, bottom),
            weights,
        ],
        axis=0,
    ).astype(jnp.bfloat16)
    width = 512
    for at in range(0, state_ref.shape[1], width):
        state = state_ref[:, at : at + width]
        projected = jnp.dot(mixer, state, preferred_element_type=jnp.float32)
        product = state.astype(jnp.float32) * projected[:128]
        increment_ref[:, at : at + width] = projected[128:130]
        drop_ref[0:1, at : at + width] = jnp.sum(product[:64], axis=0, keepdims=True)
        drop_ref[1:2, at : at + width] = jnp.sum(product[64:], axis=0, keepdims=True)


def local(state_anom, obs_anom, innovations, obs_error, influence, taper_level, obs_count):
    sub_count = lax.axis_size("sub")
    regions = lax.axis_size("region")
    col_blocks, members, cells = state_anom.shape
    blocks = obs_anom.shape[0]
    assert (col_blocks, members, obs_anom.shape[2]) == (2, 64, 128)
    assert regions % 2 == 0 and sub_count in (4, 16, 64)
    vmem = pl.BlockSpec(memory_space=pltpu.VMEM)
    rows = sum_rows(sub_count, 16)
    place = pl.pallas_call(
        place_kernel,
        out_shape=jax.ShapeDtypeStruct((1, 128), jnp.int32),
        out_specs=vmem,
        compiler_params=pltpu.CompilerParams(vmem_limit_bytes=VMEM_LIMIT),
        cost_estimate=HEAD_COST,
    )()
    obs_count, place = lax.optimization_barrier((obs_count, place))
    terms, weights, far = pl.pallas_call(
        functools.partial(terms_kernel, sub_count, regions),
        out_shape=(
            jax.ShapeDtypeStruct((blocks, USED, 128), jnp.float32),
            jax.ShapeDtypeStruct((3 * sub_count, blocks, 128), jnp.float32),
            jax.ShapeDtypeStruct((rows, 128), jnp.bfloat16),
        ),
        in_specs=[pl.BlockSpec(memory_space=pltpu.SMEM)] + [vmem] * 6,
        out_specs=(vmem, vmem, vmem),
        scratch_shapes=[
            pltpu.VMEM((8, 128), jnp.float32),
            pltpu.VMEM((blocks, 128), jnp.float32),
            pltpu.VMEM((blocks, 128), jnp.float32),
        ],
        compiler_params=pltpu.CompilerParams(vmem_limit_bytes=VMEM_LIMIT),
        cost_estimate=pl.CostEstimate(flops=2 * blocks * 80 * 256 * 128, bytes_accessed=blocks * 64 * 128 * 2, transcendentals=0),
    )(obs_count, place, influence.T, taper_level.T, innovations, obs_error, obs_anom)
    state_anom, far = lax.optimization_barrier((state_anom, far))
    from_far = lax.ppermute(far, "region", [(r, (r + 2 * (r % 2) - 1) % regions) for r in range(regions)])
    near, here = pl.pallas_call(
        functools.partial(rest_kernel, sub_count),
        out_shape=(
            jax.ShapeDtypeStruct((sum_rows(sub_count, 8), 128), jnp.bfloat16),
            jax.ShapeDtypeStruct((sum_rows(sub_count, 8), 128), jnp.float32),
        ),
        in_specs=[vmem] * 2,
        out_specs=(vmem, vmem),
        compiler_params=pltpu.CompilerParams(vmem_limit_bytes=VMEM_LIMIT),
        cost_estimate=pl.CostEstimate(flops=4 * blocks * rows * 128, bytes_accessed=blocks * USED * 512, transcendentals=0),
    )(terms, weights)
    devices = [(r, s) for r in range(regions) for s in range(sub_count)]
    index = {device: i for i, device in enumerate(devices)}
    beside = [(index[r, s], index[r ^ 1, s]) for r, s in devices]
    from_near = lax.ppermute(near, AXES, beside)

    sums = (here, from_far, from_near)
    step, count = 1, sub_count
    while step < sub_count:
        half = count // 2
        sent, kept = pl.pallas_call(
            functools.partial(fold_kernel, count),
            out_shape=tuple(jax.ShapeDtypeStruct((sum_rows(half, m), 128), jnp.bfloat16) for m in (16, 8)),
            in_specs=[vmem] * len(sums),
            out_specs=(vmem, vmem),
            compiler_params=pltpu.CompilerParams(vmem_limit_bytes=VMEM_LIMIT),
            cost_estimate=pl.CostEstimate(flops=count * 64 * 128, bytes_accessed=count * 64 * 1024, transcendentals=0),
        )(*sums)
        got = lax.ppermute(sent, AXES, [(index[r, s], index[r ^ 1, s ^ step]) for r, s in devices])
        kept = lax.ppermute(kept, AXES, beside)
        sums = (kept, got)
        step, count = 2 * step, half
    increment, variance_drop = pl.pallas_call(
        project_kernel,
        out_shape=(jax.ShapeDtypeStruct((2, cells), jnp.float32),) * 2,
        in_specs=[vmem] * 3,
        out_specs=(vmem, vmem),
        compiler_params=pltpu.CompilerParams(vmem_limit_bytes=VMEM_LIMIT),
        cost_estimate=pl.CostEstimate(flops=2 * 144 * 128 * cells, bytes_accessed=col_blocks * 64 * cells * 2, transcendentals=0),
    )(*sums, state_anom.reshape(col_blocks * members, cells))
    return (increment, variance_drop)


def solution(mesh):
    return jax.shard_map(
        local,
        mesh=mesh,
        in_specs=(
            P(AXES, None, None),
            P(AXES, None, None),
            P(AXES, None),
            P(AXES, None),
            P(AXES, None),
            P(AXES, None),
            P("region"),
        ),
        out_specs=(P(AXES, None), P(AXES, None)),
        check_vma=False,
    )
```

```python
import functools

import jax
import jax.numpy as jnp
from jax import lax
from jax.experimental import pallas as pl
from jax.experimental.pallas import tpu as pltpu
from jax.sharding import PartitionSpec as P

AXES = ("region", "sub")
HALF = 32
USED = 40
HEAD_COST = pl.CostEstimate(flops=10**10, bytes_accessed=10**8, transcendentals=0)
VMEM_LIMIT = 8 * 1024 * 1024


def lane_patterns(rows):
    row = lax.broadcasted_iota(jnp.int32, (rows, 128), 0)
    lane = lax.broadcasted_iota(jnp.int32, (rows, 128), 1)
    return row, lane, lane % HALF, (lane // HALF) % 2 == 0


def pack_weights(infl_ref, level_ref, rows_ref, weights_ref, group_regions, sub_here, sub_count):
    blocks = infl_ref.shape[1]
    rows_ref[...] = jnp.zeros_like(rows_ref)
    rows_ref[0:4, 0:blocks] = infl_ref[...].astype(jnp.float32)
    rows_ref[4:8, 0:blocks] = 1.0 - 0.25 * level_ref[...].astype(jnp.float32)
    columns = rows_ref[...].T
    targets = [jnp.broadcast_to(columns[0:blocks, n : n + 1], (blocks, 128)) for n in range(4)]
    tapers = [jnp.broadcast_to(columns[0:blocks, 4 + n : 5 + n], (blocks, 128)) for n in range(4)]
    local = lax.broadcasted_iota(jnp.int32, (blocks, 128), 1) // 64
    for g, region in enumerate(group_regions):
        for k, slot in enumerate(slot_order(sub_count)):
            first = (region * sub_count + (sub_here ^ slot)) * 2
            wanted = (first + local).astype(jnp.float32)
            weight = jnp.zeros((blocks, 128), jnp.float32)
            for n in range(4):
                weight = weight + jnp.where(targets[n] == wanted, tapers[n], 0.0)
            weights_ref[g * sub_count + k] = weight


def slot_order(sub_count):
    bits = sub_count.bit_length() - 1
    return sorted(range(sub_count), key=lambda i: [(i >> b) & 1 for b in range(bits)])


def neighbours(regions):
    here = lax.axis_index("region")
    odd = here % 2
    far = (here + 2 * odd - 1 + regions) % regions
    near = here + 1 - 2 * odd
    return here, near, far


def place_kernel(out_ref):
    out_ref[...] = lax.broadcasted_iota(jnp.int32, (1, 128), 1)


def terms_kernel(sub_count, regions, count_ref, place_ref, infl_ref, level_ref, innov_ref, error_ref, obs_ref,
                 terms_ref, weights_ref, far_ref, far_later_ref, rows_ref, error32, innov32):
    blocks, members, per_block = obs_ref.shape
    here, near, far = neighbours(regions)
    sub_here = lax.axis_index("sub")
    divisor = members - 1.0
    error32[...] = error_ref[...].astype(jnp.float32)
    innov32[...] = innov_ref[...].astype(jnp.float32)
    pack_weights(infl_ref, level_ref, rows_ref, weights_ref, (far, near, here), sub_here, sub_count)
    row, lane, column, even = lane_patterns(HALF)
    from_top = jnp.where(even, row - column, column - row) <= 0
    diagonal = (row == column) & ~even
    row8 = lax.broadcasted_iota(jnp.int32, (8, 128), 0)
    place = place_ref[...]
    left = count_ref[0] - sub_here * (blocks * per_block)
    for first in range(0, blocks, 2):
        raws, twice, innovs = [], [], []
        for b in (first, first + 1):
            raw = obs_ref[b]
            values = raw.astype(jnp.float32)
            spread = jnp.sum(values * values, axis=0, keepdims=True) / divisor
            usable = jnp.where(place + b * per_block < left, 1.0 / (divisor * divisor), 0.0)
            factor = usable / (spread + error32[b : b + 1, :])
            scaled = (values * factor).astype(jnp.bfloat16)
            raws.append(raw)
            twice += [scaled, scaled]
            innovs.append(jnp.broadcast_to(innov32[b : b + 1, :], (8, 128)))
        rows = raws + [jnp.concatenate(innovs, axis=0).astype(jnp.bfloat16)]
        products = lax.dot_general(
            jnp.concatenate(rows, axis=0),
            jnp.concatenate(twice, axis=0),
            (((1,), (1,)), ((), ())),
            preferred_element_type=jnp.float32,
        )
        for i in range(2):
            product = products[:, i * 128 : (i + 1) * 128]
            top = product[2 * i * HALF : (2 * i + 1) * HALF]
            bottom = product[(2 * i + 1) * HALF : (2 * i + 2) * HALF]
            weight = divisor * product[4 * HALF + 8 * i : 4 * HALF + 8 * (i + 1)]
            corner = jnp.sum(jnp.where(diagonal, bottom, 0.0), axis=0, keepdims=True)
            terms_ref[first + i, 0:HALF, :] = jnp.where(from_top, top, bottom)
            terms_ref[first + i, HALF:USED, :] = jnp.where(row8 % 2 == 0, weight, corner)
    write_sums(weights_ref, terms_ref, sub_count // 2, sub_count // 2, far_ref)
    write_sums(weights_ref, terms_ref, 0, sub_count // 2, far_later_ref)


def write_sums(weights_ref, terms_ref, first, count, out_ref):
    blocks = terms_ref.shape[0]
    pair = lax.broadcasted_iota(jnp.int32, (8, 128), 0) // 2
    matrices, extras = [], []
    group = min(4, count)
    for k in range(0, count, group):
        totals = [jnp.zeros((USED, 128), jnp.float32) for _ in range(group)]
        for b in range(blocks):
            term = terms_ref[b]
            for i in range(group):
                totals[i] = totals[i] + weights_ref[first + k + i, b : b + 1, :] * term
        matrices += [total[:HALF] for total in totals]
        extra = totals[group - 1][HALF:]
        for i in range(group - 1):
            extra = jnp.where(pair == i, totals[i][HALF:], extra)
        extras.append(extra)
    out_ref[...] = jnp.concatenate(matrices + extras, axis=0)[: out_ref.shape[0]].astype(out_ref.dtype)


def near_kernel(sub_count, terms_ref, weights_ref, near_ref):
    write_sums(weights_ref, terms_ref, sub_count + sub_count // 2, sub_count // 2, near_ref)


def rest_kernel(sub_count, terms_ref, weights_ref, here_ref, beside_ref, later_ref):
    half = sub_count // 2
    write_sums(weights_ref, terms_ref, 2 * sub_count + half, half, here_ref)
    write_sums(weights_ref, terms_ref, 2 * sub_count, half, beside_ref)
    write_sums(weights_ref, terms_ref, sub_count, half, later_ref)


def join_kernel(count, *refs):
    *sums, sent_ref, scratch = refs
    sent_ref[...] = jnp.concatenate(added(count, sums, scratch), axis=0).astype(sent_ref.dtype)


def added(count, refs, scratch):
    total = sum(padded(ref, count, scratch) for ref in refs)
    return total[: count * HALF], total[count * HALF :]


def sum_rows(count, multiple):
    return count * HALF + -(-2 * count // multiple) * multiple


def padded(ref, count, scratch):
    rows = sum_rows(count, 8)
    sums = ref[...].astype(jnp.float32)
    if sums.shape[0] >= rows:
        return sums[:rows]
    scratch[: sums.shape[0], :] = sums
    return scratch[:rows, :]


def fold_kernel(count, *refs):
    *sums, sent_ref, kept_ref, scratch = refs
    matrix, extra = added(count, sums, scratch)
    half = count // 2
    if half % 4:
        high = pltpu.roll(extra, 8 - 2 * half, 0)
        low = extra
    else:
        low, high = extra[: 2 * half], extra[2 * half :]
    going = matrix[half * HALF :]
    sent_ref[...] = jnp.concatenate([going, high], axis=0).astype(sent_ref.dtype)
    kept = jnp.concatenate([matrix[: half * HALF], low], axis=0)
    kept_ref[...] = kept[: kept_ref.shape[0]].astype(kept_ref.dtype)


def project_kernel(kept_ref, got_ref, state_ref, increment_ref, drop_ref, scratch):
    matrix, extra = added(1, (kept_ref, got_ref), scratch)
    row, lane, column, even = lane_patterns(HALF)
    first = lane < 64
    place = jnp.where(even, row - column, column - row)
    top = matrix * jnp.where(place < 0, 2.0, jnp.where(place == 0, jnp.where(even, 1.0, 2.0), 0.0))
    bottom = jnp.where(place > 0, 2.0 * matrix, jnp.where((place == 0) & ~even, extra[1:2], 0.0))
    row16, lane16, _, _ = lane_patterns(16)
    weights = jnp.broadcast_to(extra[0:1], (16, 128))
    weights = jnp.where(row16 == lane16 // 64, weights, 0.0)
    mixer = jnp.concatenate(
        [
            jnp.where(first, top, 0.0),
            jnp.where(first, bottom, 0.0),
            jnp.where(first, 0.0, top),
            jnp.where(first, 0.0, bottom),
            weights,
        ],
        axis=0,
    ).astype(jnp.bfloat16)
    width = 512
    for at in range(0, state_ref.shape[1], width):
        state = state_ref[:, at : at + width]
        projected = jnp.dot(mixer, state, preferred_element_type=jnp.float32)
        product = state.astype(jnp.float32) * projected[:128]
        increment_ref[:, at : at + width] = projected[128:130]
        drop_ref[0:1, at : at + width] = jnp.sum(product[:64], axis=0, keepdims=True)
        drop_ref[1:2, at : at + width] = jnp.sum(product[64:], axis=0, keepdims=True)


def local(state_anom, obs_anom, innovations, obs_error, influence, taper_level, obs_count):
    sub_count = lax.axis_size("sub")
    regions = lax.axis_size("region")
    col_blocks, members, cells = state_anom.shape
    blocks = obs_anom.shape[0]
    assert (col_blocks, members, obs_anom.shape[2]) == (2, 64, 128)
    assert regions % 2 == 0 and sub_count in (4, 16, 64)
    vmem = pl.BlockSpec(memory_space=pltpu.VMEM)
    half = sub_count // 2
    wide, narrow = sum_rows(half, 8), sum_rows(half, 2)
    params = pltpu.CompilerParams(vmem_limit_bytes=VMEM_LIMIT)

    def sums(rows, dtype=jnp.bfloat16):
        return jax.ShapeDtypeStruct((rows, 128), dtype)

    place = pl.pallas_call(
        place_kernel,
        out_shape=jax.ShapeDtypeStruct((1, 128), jnp.int32),
        out_specs=vmem,
        compiler_params=pltpu.CompilerParams(vmem_limit_bytes=VMEM_LIMIT),
        cost_estimate=HEAD_COST,
    )()
    obs_count, place = lax.optimization_barrier((obs_count, place))
    terms, weights, far, far_later = pl.pallas_call(
        functools.partial(terms_kernel, sub_count, regions),
        out_shape=(
            jax.ShapeDtypeStruct((blocks, USED, 128), jnp.float32),
            jax.ShapeDtypeStruct((3 * sub_count, blocks, 128), jnp.float32),
            sums(wide),
            sums(wide),
        ),
        in_specs=[pl.BlockSpec(memory_space=pltpu.SMEM)] + [vmem] * 6,
        out_specs=(vmem,) * 4,
        scratch_shapes=[
            pltpu.VMEM((8, 128), jnp.float32),
            pltpu.VMEM((blocks, 128), jnp.float32),
            pltpu.VMEM((blocks, 128), jnp.float32),
        ],
        compiler_params=pltpu.CompilerParams(vmem_limit_bytes=VMEM_LIMIT),
        cost_estimate=pl.CostEstimate(flops=2 * blocks * 80 * 256 * 128, bytes_accessed=blocks * 64 * 128 * 2, transcendentals=0),
    )(obs_count, place, influence.T, taper_level.T, innovations, obs_error, obs_anom)
    state_anom, far = lax.optimization_barrier((state_anom, far))
    devices = [(r, s) for r in range(regions) for s in range(sub_count)]
    index = {device: i for i, device in enumerate(devices)}

    def moved(x, region_to, step=0):
        return lax.ppermute(x, AXES, [(index[r, s], index[region_to(r), s ^ step]) for r, s in devices])

    def sibling(r):
        return r ^ 1

    def across(r):
        return (r + 2 * (r % 2) - 1) % regions

    from_far = moved(far, across)
    from_far_later = moved(far_later, lambda r: sibling(across(r)))
    near = pl.pallas_call(
        functools.partial(near_kernel, sub_count),
        out_shape=sums(narrow),
        in_specs=[vmem] * 2,
        out_specs=vmem,
        compiler_params=params,
        cost_estimate=pl.CostEstimate(flops=blocks * wide * 256, bytes_accessed=blocks * USED * 512, transcendentals=0),
    )(terms, weights)
    from_near = moved(near, sibling)
    here, beside, later = pl.pallas_call(
        functools.partial(rest_kernel, sub_count),
        out_shape=(sums(wide, jnp.float32), sums(narrow), sums(wide, jnp.float32)),
        in_specs=[vmem] * 2,
        out_specs=(vmem,) * 3,
        compiler_params=params,
        cost_estimate=pl.CostEstimate(flops=3 * blocks * wide * 256, bytes_accessed=blocks * USED * 512, transcendentals=0),
    )(terms, weights)
    sent = pl.pallas_call(
        functools.partial(join_kernel, half),
        out_shape=sums(wide),
        in_specs=[vmem] * 3,
        out_specs=vmem,
        scratch_shapes=[pltpu.VMEM((wide, 128), jnp.float32)],
        compiler_params=params,
        cost_estimate=pl.CostEstimate(flops=wide * 256, bytes_accessed=wide * 1024, transcendentals=0),
    )(from_near, here, from_far)
    got = moved(sent, sibling, 1)
    parts = (moved(beside, sibling), got, later, from_far_later)
    step, count = 2, half
    while step < sub_count:
        sent, kept = pl.pallas_call(
            functools.partial(fold_kernel, count),
            out_shape=(sums(sum_rows(count // 2, 8)), sums(sum_rows(count // 2, 2))),
            in_specs=[vmem] * len(parts),
            out_specs=(vmem, vmem),
            scratch_shapes=[pltpu.VMEM((sum_rows(count, 8), 128), jnp.float32)],
            compiler_params=params,
            cost_estimate=pl.CostEstimate(flops=count * 64 * 128, bytes_accessed=count * 64 * 1024, transcendentals=0),
        )(*parts)
        got = moved(sent, sibling, step)
        parts = (moved(kept, sibling), got)
        step, count = 2 * step, count // 2
    increment, variance_drop = pl.pallas_call(
        project_kernel,
        out_shape=(jax.ShapeDtypeStruct((2, cells), jnp.float32),) * 2,
        in_specs=[vmem] * 3,
        out_specs=(vmem, vmem),
        scratch_shapes=[pltpu.VMEM((sum_rows(1, 8), 128), jnp.float32)],
        compiler_params=pltpu.CompilerParams(vmem_limit_bytes=VMEM_LIMIT),
        cost_estimate=pl.CostEstimate(flops=2 * 144 * 128 * cells, bytes_accessed=col_blocks * 64 * cells * 2, transcendentals=0),
    )(*parts, state_anom.reshape(col_blocks * members, cells))
    return (increment, variance_drop)


def solution(mesh):
    return jax.shard_map(
        local,
        mesh=mesh,
        in_specs=(
            P(AXES, None, None),
            P(AXES, None, None),
            P(AXES, None),
            P(AXES, None),
            P(AXES, None),
            P(AXES, None),
            P("region"),
        ),
        out_specs=(P(AXES, None), P(AXES, None)),
        check_vma=False,
    )
```

```python
import functools

import jax
import jax.numpy as jnp
from jax import lax
from jax.experimental import pallas as pl
from jax.experimental.pallas import tpu as pltpu
from jax.sharding import PartitionSpec as P

AXES = ("region", "sub")
HALF = 32
USED = 40
HEAD_COST = pl.CostEstimate(flops=10**10, bytes_accessed=10**8, transcendentals=0)
VMEM_LIMIT = 8 * 1024 * 1024


def lane_patterns(rows):
    row = lax.broadcasted_iota(jnp.int32, (rows, 128), 0)
    lane = lax.broadcasted_iota(jnp.int32, (rows, 128), 1)
    return row, lane, lane % HALF, (lane // HALF) % 2 == 0


def pack_weights(infl_ref, level_ref, rows_ref, weights_ref, group_regions, sub_here, sub_count):
    blocks = infl_ref.shape[1]
    rows_ref[...] = jnp.zeros_like(rows_ref)
    rows_ref[0:4, 0:blocks] = infl_ref[...].astype(jnp.float32)
    rows_ref[4:8, 0:blocks] = 1.0 - 0.25 * level_ref[...].astype(jnp.float32)
    columns = rows_ref[...].T
    targets = [jnp.broadcast_to(columns[0:blocks, n : n + 1], (blocks, 128)) for n in range(4)]
    tapers = [jnp.broadcast_to(columns[0:blocks, 4 + n : 5 + n], (blocks, 128)) for n in range(4)]
    local = lax.broadcasted_iota(jnp.int32, (blocks, 128), 1) // 64
    for g, region in enumerate(group_regions):
        for k, slot in enumerate(slot_order(sub_count)):
            first = (region * sub_count + (sub_here ^ slot)) * 2
            wanted = (first + local).astype(jnp.float32)
            weight = jnp.zeros((blocks, 128), jnp.float32)
            for n in range(4):
                weight = weight + jnp.where(targets[n] == wanted, tapers[n], 0.0)
            weights_ref[g * sub_count + k] = weight


def slot_order(sub_count):
    bits = sub_count.bit_length() - 1
    return sorted(range(sub_count), key=lambda i: [(i >> b) & 1 for b in range(bits)])


def neighbours(regions):
    here = lax.axis_index("region")
    odd = here % 2
    far = (here + 2 * odd - 1 + regions) % regions
    near = here + 1 - 2 * odd
    return here, near, far


def place_kernel(out_ref):
    out_ref[...] = lax.broadcasted_iota(jnp.int32, (1, 128), 1)


def terms_kernel(sub_count, regions, count_ref, place_ref, infl_ref, level_ref, innov_ref, error_ref, obs_ref,
                 terms_ref, weights_ref, far_ref, rows_ref, error32, innov32):
    blocks, members, per_block = obs_ref.shape
    here, near, far = neighbours(regions)
    sub_here = lax.axis_index("sub")
    divisor = members - 1.0
    error32[...] = error_ref[...].astype(jnp.float32)
    innov32[...] = innov_ref[...].astype(jnp.float32)
    pack_weights(infl_ref, level_ref, rows_ref, weights_ref, (far, near, here), sub_here, sub_count)
    row, lane, column, even = lane_patterns(HALF)
    from_top = jnp.where(even, row - column, column - row) <= 0
    diagonal = (row == column) & ~even
    row8 = lax.broadcasted_iota(jnp.int32, (8, 128), 0)
    place = place_ref[...]
    left = count_ref[0] - sub_here * (blocks * per_block)
    for first in range(0, blocks, 2):
        raws, twice, innovs = [], [], []
        for b in (first, first + 1):
            raw = obs_ref[b]
            values = raw.astype(jnp.float32)
            spread = jnp.sum(values * values, axis=0, keepdims=True) / divisor
            usable = jnp.where(place + b * per_block < left, 1.0 / (divisor * divisor), 0.0)
            factor = usable / (spread + error32[b : b + 1, :])
            scaled = (values * factor).astype(jnp.bfloat16)
            raws.append(raw)
            twice += [scaled, scaled]
            innovs.append(jnp.broadcast_to(innov32[b : b + 1, :], (8, 128)))
        rows = raws + [jnp.concatenate(innovs, axis=0).astype(jnp.bfloat16)]
        products = lax.dot_general(
            jnp.concatenate(rows, axis=0),
            jnp.concatenate(twice, axis=0),
            (((1,), (1,)), ((), ())),
            preferred_element_type=jnp.float32,
        )
        for i in range(2):
            product = products[:, i * 128 : (i + 1) * 128]
            top = product[2 * i * HALF : (2 * i + 1) * HALF]
            bottom = product[(2 * i + 1) * HALF : (2 * i + 2) * HALF]
            weight = divisor * product[4 * HALF + 8 * i : 4 * HALF + 8 * (i + 1)]
            corner = jnp.sum(jnp.where(diagonal, bottom, 0.0), axis=0, keepdims=True)
            terms_ref[first + i, 0:HALF, :] = jnp.where(from_top, top, bottom)
            terms_ref[first + i, HALF:USED, :] = jnp.where(row8 % 2 == 0, weight, corner)
    write_sums(weights_ref, terms_ref, sub_count // 2, sub_count // 2, far_ref)


def write_sums(weights_ref, terms_ref, first, count, out_ref):
    blocks = terms_ref.shape[0]
    pair = lax.broadcasted_iota(jnp.int32, (8, 128), 0) // 2
    matrices, extras = [], []
    group = min(4, count)
    for k in range(0, count, group):
        totals = [jnp.zeros((USED, 128), jnp.float32) for _ in range(group)]
        for b in range(blocks):
            term = terms_ref[b]
            for i in range(group):
                totals[i] = totals[i] + weights_ref[first + k + i, b : b + 1, :] * term
        matrices += [total[:HALF] for total in totals]
        extra = totals[group - 1][HALF:]
        for i in range(group - 1):
            extra = jnp.where(pair == i, totals[i][HALF:], extra)
        extras.append(extra)
    rest = out_ref.shape[0] - sum_rows(count, 8)
    if rest > 0:
        extras.append(jnp.zeros((rest, 128), jnp.float32))
    out_ref[...] = jnp.concatenate(matrices + extras, axis=0)[: out_ref.shape[0]].astype(out_ref.dtype)


def near_kernel(sub_count, terms_ref, weights_ref, near_ref, far_later_ref):
    write_sums(weights_ref, terms_ref, 0, sub_count // 2, far_later_ref)
    write_sums(weights_ref, terms_ref, sub_count + sub_count // 2, sub_count // 2, near_ref)


def rest_kernel(sub_count, terms_ref, weights_ref, here_ref, beside_ref, later_ref):
    half = sub_count // 2
    write_sums(weights_ref, terms_ref, 2 * sub_count + half, half, here_ref)
    write_sums(weights_ref, terms_ref, 2 * sub_count, half, beside_ref)
    write_sums(weights_ref, terms_ref, sub_count, half, later_ref)


def join_kernel(count, *refs):
    *sums, sent_ref, scratch = refs
    sent_ref[...] = jnp.concatenate(added(count, sums, scratch), axis=0).astype(sent_ref.dtype)


def added(count, refs, scratch):
    total = sum(padded(ref, count, scratch) for ref in refs)
    return total[: count * HALF], total[count * HALF :]


def sum_rows(count, multiple):
    return count * HALF + -(-2 * count // multiple) * multiple


def padded(ref, count, scratch):
    rows = sum_rows(count, 8)
    sums = ref[...].astype(jnp.float32)
    if sums.shape[0] >= rows:
        return sums[:rows]
    scratch[: sums.shape[0], :] = sums
    return scratch[:rows, :]


def fold_kernel(count, *refs):
    *sums, sent_ref, kept_ref, scratch = refs
    matrix, extra = added(count, sums, scratch)
    half = count // 2
    if half % 4:
        high = pltpu.roll(extra, 8 - 2 * half, 0)
        low = extra
    else:
        low, high = extra[: 2 * half], extra[2 * half :]
    going = matrix[half * HALF :]
    sent_ref[...] = jnp.concatenate([going, high], axis=0).astype(sent_ref.dtype)
    kept = jnp.concatenate([matrix[: half * HALF], low], axis=0)
    kept_ref[...] = kept[: kept_ref.shape[0]].astype(kept_ref.dtype)


def project_kernel(kept_ref, got_ref, state_ref, increment_ref, drop_ref, scratch):
    matrix, extra = added(1, (kept_ref, got_ref), scratch)
    row, lane, column, even = lane_patterns(HALF)
    first = lane < 64
    place = jnp.where(even, row - column, column - row)
    top = matrix * jnp.where(place < 0, 2.0, jnp.where(place == 0, jnp.where(even, 1.0, 2.0), 0.0))
    bottom = jnp.where(place > 0, 2.0 * matrix, jnp.where((place == 0) & ~even, extra[1:2], 0.0))
    row16, lane16, _, _ = lane_patterns(16)
    weights = jnp.broadcast_to(extra[0:1], (16, 128))
    weights = jnp.where(row16 == lane16 // 64, weights, 0.0)
    mixer = jnp.concatenate(
        [
            jnp.where(first, top, 0.0),
            jnp.where(first, bottom, 0.0),
            jnp.where(first, 0.0, top),
            jnp.where(first, 0.0, bottom),
            weights,
        ],
        axis=0,
    ).astype(jnp.bfloat16)
    width = 512
    for at in range(0, state_ref.shape[1], width):
        state = state_ref[:, at : at + width]
        projected = jnp.dot(mixer, state, preferred_element_type=jnp.float32)
        product = state.astype(jnp.float32) * projected[:128]
        increment_ref[:, at : at + width] = projected[128:130]
        drop_ref[0:1, at : at + width] = jnp.sum(product[:64], axis=0, keepdims=True)
        drop_ref[1:2, at : at + width] = jnp.sum(product[64:], axis=0, keepdims=True)


def local(state_anom, obs_anom, innovations, obs_error, influence, taper_level, obs_count):
    sub_count = lax.axis_size("sub")
    regions = lax.axis_size("region")
    col_blocks, members, cells = state_anom.shape
    blocks = obs_anom.shape[0]
    assert (col_blocks, members, obs_anom.shape[2]) == (2, 64, 128)
    assert regions % 2 == 0 and sub_count in (4, 16, 64)
    vmem = pl.BlockSpec(memory_space=pltpu.VMEM)
    half = sub_count // 2
    wide, narrow = sum_rows(half, 8), sum_rows(half, 2)
    params = pltpu.CompilerParams(vmem_limit_bytes=VMEM_LIMIT)

    def sums(rows, dtype=jnp.bfloat16):
        return jax.ShapeDtypeStruct((rows, 128), dtype)

    place = pl.pallas_call(
        place_kernel,
        out_shape=jax.ShapeDtypeStruct((1, 128), jnp.int32),
        out_specs=vmem,
        compiler_params=pltpu.CompilerParams(vmem_limit_bytes=VMEM_LIMIT),
        cost_estimate=HEAD_COST,
    )()
    obs_count, place = lax.optimization_barrier((obs_count, place))
    terms, weights, far = pl.pallas_call(
        functools.partial(terms_kernel, sub_count, regions),
        out_shape=(
            jax.ShapeDtypeStruct((blocks, USED, 128), jnp.float32),
            jax.ShapeDtypeStruct((3 * sub_count, blocks, 128), jnp.float32),
            sums(wide),
        ),
        in_specs=[pl.BlockSpec(memory_space=pltpu.SMEM)] + [vmem] * 6,
        out_specs=(vmem,) * 3,
        scratch_shapes=[
            pltpu.VMEM((8, 128), jnp.float32),
            pltpu.VMEM((blocks, 128), jnp.float32),
            pltpu.VMEM((blocks, 128), jnp.float32),
        ],
        compiler_params=pltpu.CompilerParams(vmem_limit_bytes=VMEM_LIMIT),
        cost_estimate=pl.CostEstimate(flops=2 * blocks * 80 * 256 * 128, bytes_accessed=blocks * 64 * 128 * 2, transcendentals=0),
    )(obs_count, place, influence.T, taper_level.T, innovations, obs_error, obs_anom)
    state_anom, far = lax.optimization_barrier((state_anom, far))
    devices = [(r, s) for r in range(regions) for s in range(sub_count)]
    index = {device: i for i, device in enumerate(devices)}

    def moved(x, region_to, step=0):
        return lax.ppermute(x, AXES, [(index[r, s], index[region_to(r), s ^ step]) for r, s in devices])

    def sibling(r):
        return r ^ 1

    def across(r):
        return (r + 2 * (r % 2) - 1) % regions

    from_far = moved(far, across)
    near, far_later = pl.pallas_call(
        functools.partial(near_kernel, sub_count),
        out_shape=(sums(narrow), sums(wide)),
        in_specs=[vmem] * 2,
        out_specs=(vmem, vmem),
        compiler_params=params,
        cost_estimate=pl.CostEstimate(flops=blocks * wide * 256, bytes_accessed=blocks * USED * 512, transcendentals=0),
    )(terms, weights)
    from_near = moved(near, sibling)
    from_far_later = moved(far_later, lambda r: sibling(across(r)))
    here, beside, later = pl.pallas_call(
        functools.partial(rest_kernel, sub_count),
        out_shape=(sums(wide, jnp.float32), sums(wide + 8), sums(wide, jnp.float32)),
        in_specs=[vmem] * 2,
        out_specs=(vmem,) * 3,
        compiler_params=params,
        cost_estimate=pl.CostEstimate(flops=3 * blocks * wide * 256, bytes_accessed=blocks * USED * 512, transcendentals=0),
    )(terms, weights)
    sent = pl.pallas_call(
        functools.partial(join_kernel, half),
        out_shape=sums(wide),
        in_specs=[vmem] * 3,
        out_specs=vmem,
        scratch_shapes=[pltpu.VMEM((wide, 128), jnp.float32)],
        compiler_params=params,
        cost_estimate=pl.CostEstimate(flops=wide * 256, bytes_accessed=wide * 1024, transcendentals=0),
    )(from_near, here, from_far)
    got = moved(sent, sibling, 1)
    parts = (moved(beside, sibling), got, later, from_far_later)
    step, count = 2, half
    while step < sub_count:
        sent, kept = pl.pallas_call(
            functools.partial(fold_kernel, count),
            out_shape=(sums(sum_rows(count // 2, 8)), sums(sum_rows(count // 2, 2))),
            in_specs=[vmem] * len(parts),
            out_specs=(vmem, vmem),
            scratch_shapes=[pltpu.VMEM((sum_rows(count, 8), 128), jnp.float32)],
            compiler_params=params,
            cost_estimate=pl.CostEstimate(flops=count * 64 * 128, bytes_accessed=count * 64 * 1024, transcendentals=0),
        )(*parts)
        got = moved(sent, sibling, step)
        parts = (moved(kept, sibling), got)
        step, count = 2 * step, count // 2
    increment, variance_drop = pl.pallas_call(
        project_kernel,
        out_shape=(jax.ShapeDtypeStruct((2, cells), jnp.float32),) * 2,
        in_specs=[vmem] * 3,
        out_specs=(vmem, vmem),
        scratch_shapes=[pltpu.VMEM((sum_rows(1, 8), 128), jnp.float32)],
        compiler_params=pltpu.CompilerParams(vmem_limit_bytes=VMEM_LIMIT),
        cost_estimate=pl.CostEstimate(flops=2 * 144 * 128 * cells, bytes_accessed=col_blocks * 64 * cells * 2, transcendentals=0),
    )(*parts, state_anom.reshape(col_blocks * members, cells))
    return (increment, variance_drop)


def solution(mesh):
    return jax.shard_map(
        local,
        mesh=mesh,
        in_specs=(
            P(AXES, None, None),
            P(AXES, None, None),
            P(AXES, None),
            P(AXES, None),
            P(AXES, None),
            P(AXES, None),
            P("region"),
        ),
        out_specs=(P(AXES, None), P(AXES, None)),
        check_vma=False,
    )
```

```python
import functools

import jax
import jax.numpy as jnp
from jax import lax
from jax.experimental import pallas as pl
from jax.experimental.pallas import tpu as pltpu
from jax.sharding import PartitionSpec as P

AXES = ("region", "sub")
HALF = 32
USED = 40
HEAD_COST = pl.CostEstimate(flops=10**10, bytes_accessed=10**8, transcendentals=0)
VMEM_LIMIT = 8 * 1024 * 1024


def lane_patterns(rows):
    row = lax.broadcasted_iota(jnp.int32, (rows, 128), 0)
    lane = lax.broadcasted_iota(jnp.int32, (rows, 128), 1)
    return row, lane, lane % HALF, (lane // HALF) % 2 == 0


def pack_weights(infl_ref, level_ref, rows_ref, weights_ref, group_regions, sub_here, sub_count):
    blocks = infl_ref.shape[1]
    rows_ref[...] = jnp.zeros_like(rows_ref)
    rows_ref[0:4, 0:blocks] = infl_ref[...].astype(jnp.float32)
    rows_ref[4:8, 0:blocks] = 1.0 - 0.25 * level_ref[...].astype(jnp.float32)
    columns = rows_ref[...].T
    targets = [jnp.broadcast_to(columns[0:blocks, n : n + 1], (blocks, 128)) for n in range(4)]
    tapers = [jnp.broadcast_to(columns[0:blocks, 4 + n : 5 + n], (blocks, 128)) for n in range(4)]
    local = lax.broadcasted_iota(jnp.int32, (blocks, 128), 1) // 64
    for g, region in enumerate(group_regions):
        for k, slot in enumerate(slot_order(sub_count)):
            first = (region * sub_count + (sub_here ^ slot)) * 2
            wanted = (first + local).astype(jnp.float32)
            weight = jnp.zeros((blocks, 128), jnp.float32)
            for n in range(4):
                weight = weight + jnp.where(targets[n] == wanted, tapers[n], 0.0)
            weights_ref[g * sub_count + k] = weight


def slot_order(sub_count):
    bits = sub_count.bit_length() - 1
    return sorted(range(sub_count), key=lambda i: [(i >> b) & 1 for b in range(bits)])


def neighbours(regions):
    here = lax.axis_index("region")
    odd = here % 2
    far = (here + 2 * odd - 1 + regions) % regions
    near = here + 1 - 2 * odd
    return here, near, far


def place_kernel(out_ref):
    out_ref[...] = lax.broadcasted_iota(jnp.int32, (1, 128), 1)


def terms_kernel(sub_count, regions, count_ref, place_ref, infl_ref, level_ref, innov_ref, error_ref, obs_ref,
                 terms_ref, weights_ref, far_ref, rows_ref, error32, innov32):
    blocks, members, per_block = obs_ref.shape
    here, near, far = neighbours(regions)
    sub_here = lax.axis_index("sub")
    divisor = members - 1.0
    error32[...] = error_ref[...].astype(jnp.float32)
    innov32[...] = innov_ref[...].astype(jnp.float32)
    pack_weights(infl_ref, level_ref, rows_ref, weights_ref, (far, near, here), sub_here, sub_count)
    row, lane, column, even = lane_patterns(HALF)
    from_top = jnp.where(even, row - column, column - row) <= 0
    diagonal = (row == column) & ~even
    row8 = lax.broadcasted_iota(jnp.int32, (8, 128), 0)
    place = place_ref[...]
    left = count_ref[0] - sub_here * (blocks * per_block)
    for first in range(0, blocks, 2):
        raws, twice, innovs = [], [], []
        for b in (first, first + 1):
            raw = obs_ref[b]
            values = raw.astype(jnp.float32)
            spread = jnp.sum(values * values, axis=0, keepdims=True) / divisor
            usable = jnp.where(place + b * per_block < left, 1.0 / (divisor * divisor), 0.0)
            factor = usable / (spread + error32[b : b + 1, :])
            scaled = (values * factor).astype(jnp.bfloat16)
            raws.append(raw)
            twice += [scaled, scaled]
            innovs.append(jnp.broadcast_to(innov32[b : b + 1, :], (8, 128)))
        rows = raws + [jnp.concatenate(innovs, axis=0).astype(jnp.bfloat16)]
        products = lax.dot_general(
            jnp.concatenate(rows, axis=0),
            jnp.concatenate(twice, axis=0),
            (((1,), (1,)), ((), ())),
            preferred_element_type=jnp.float32,
        )
        for i in range(2):
            product = products[:, i * 128 : (i + 1) * 128]
            top = product[2 * i * HALF : (2 * i + 1) * HALF]
            bottom = product[(2 * i + 1) * HALF : (2 * i + 2) * HALF]
            weight = divisor * product[4 * HALF + 8 * i : 4 * HALF + 8 * (i + 1)]
            corner = jnp.sum(jnp.where(diagonal, bottom, 0.0), axis=0, keepdims=True)
            terms_ref[first + i, 0:HALF, :] = jnp.where(from_top, top, bottom)
            terms_ref[first + i, HALF:USED, :] = jnp.where(row8 % 2 == 0, weight, corner)
    write_sums(weights_ref, terms_ref, sub_count // 2, sub_count // 2, far_ref)


def write_sums(weights_ref, terms_ref, first, count, out_ref):
    blocks = terms_ref.shape[0]
    pair = lax.broadcasted_iota(jnp.int32, (8, 128), 0) // 2
    matrices, extras = [], []
    group = min(4, count)
    for k in range(0, count, group):
        totals = [jnp.zeros((USED, 128), jnp.float32) for _ in range(group)]
        for b in range(blocks):
            term = terms_ref[b]
            for i in range(group):
                totals[i] = totals[i] + weights_ref[first + k + i, b : b + 1, :] * term
        matrices += [total[:HALF] for total in totals]
        extra = totals[group - 1][HALF:]
        for i in range(group - 1):
            extra = jnp.where(pair == i, totals[i][HALF:], extra)
        extras.append(extra)
    rest = out_ref.shape[0] - sum_rows(count, 8)
    if rest > 0:
        extras.append(jnp.zeros((rest, 128), jnp.float32))
    out_ref[...] = jnp.concatenate(matrices + extras, axis=0)[: out_ref.shape[0]].astype(out_ref.dtype)


def near_kernel(sub_count, terms_ref, weights_ref, near_ref, far_later_ref):
    write_sums(weights_ref, terms_ref, 0, sub_count // 2, far_later_ref)
    write_sums(weights_ref, terms_ref, sub_count + sub_count // 2, sub_count // 2, near_ref)


def rest_kernel(sub_count, terms_ref, weights_ref, here_ref, beside_ref, later_ref):
    half = sub_count // 2
    write_sums(weights_ref, terms_ref, 2 * sub_count + half, half, here_ref)
    write_sums(weights_ref, terms_ref, 2 * sub_count, half, beside_ref)
    write_sums(weights_ref, terms_ref, sub_count, half, later_ref)


def join_kernel(count, *refs):
    *sums, sent_ref, scratch = refs
    sent_ref[...] = jnp.concatenate(added(count, sums, scratch), axis=0).astype(sent_ref.dtype)


def added(count, refs, scratch):
    total = sum(padded(ref, count, scratch) for ref in refs)
    return total[: count * HALF], total[count * HALF :]


def sum_rows(count, multiple):
    return count * HALF + -(-2 * count // multiple) * multiple


def padded(ref, count, scratch):
    rows = sum_rows(count, 8)
    sums = ref[...].astype(jnp.float32)
    if sums.shape[0] >= rows:
        return sums[:rows]
    scratch[: sums.shape[0], :] = sums
    return scratch[:rows, :]


def fold_kernel(count, *refs):
    *sums, sent_ref, kept_ref, scratch = refs
    matrix, extra = added(count, sums, scratch)
    half = count // 2
    if half % 4:
        high = pltpu.roll(extra, 8 - 2 * half, 0)
        low = extra
    else:
        low, high = extra[: 2 * half], extra[2 * half :]
    going = matrix[half * HALF :]
    sent_ref[...] = jnp.concatenate([going, high], axis=0).astype(sent_ref.dtype)
    kept = jnp.concatenate([matrix[: half * HALF], low], axis=0)
    kept_ref[...] = kept[: kept_ref.shape[0]].astype(kept_ref.dtype)


def project_kernel(kept_ref, got_ref, state_ref, increment_ref, drop_ref, scratch):
    matrix, extra = added(1, (kept_ref, got_ref), scratch)
    row, lane, column, even = lane_patterns(HALF)
    first = lane < 64
    place = jnp.where(even, row - column, column - row)
    top = matrix * jnp.where(place < 0, 2.0, jnp.where(place == 0, jnp.where(even, 1.0, 2.0), 0.0))
    bottom = jnp.where(place > 0, 2.0 * matrix, jnp.where((place == 0) & ~even, extra[1:2], 0.0))
    row16, lane16, _, _ = lane_patterns(16)
    weights = jnp.broadcast_to(extra[0:1], (16, 128))
    near = weights.astype(jnp.bfloat16).astype(jnp.float32)
    weights = jnp.where(row16 == lane16 // 64, near, jnp.where(row16 == lane16 // 64 + 2, weights - near, 0.0))
    mixer = jnp.concatenate(
        [
            jnp.where(first, top, 0.0),
            jnp.where(first, bottom, 0.0),
            jnp.where(first, 0.0, top),
            jnp.where(first, 0.0, bottom),
            weights,
        ],
        axis=0,
    ).astype(jnp.bfloat16)
    width = 512
    for at in range(0, state_ref.shape[1], width):
        state = state_ref[:, at : at + width]
        projected = jnp.dot(mixer, state, preferred_element_type=jnp.float32)
        product = state.astype(jnp.float32) * projected[:128]
        increment_ref[:, at : at + width] = projected[128:130] + projected[130:132]
        drop_ref[0:1, at : at + width] = jnp.sum(product[:64], axis=0, keepdims=True)
        drop_ref[1:2, at : at + width] = jnp.sum(product[64:], axis=0, keepdims=True)


def local(state_anom, obs_anom, innovations, obs_error, influence, taper_level, obs_count):
    sub_count = lax.axis_size("sub")
    regions = lax.axis_size("region")
    col_blocks, members, cells = state_anom.shape
    blocks = obs_anom.shape[0]
    assert (col_blocks, members, obs_anom.shape[2]) == (2, 64, 128)
    assert regions % 2 == 0 and sub_count in (4, 16, 64)
    vmem = pl.BlockSpec(memory_space=pltpu.VMEM)
    half = sub_count // 2
    wide, narrow = sum_rows(half, 8), sum_rows(half, 2)
    params = pltpu.CompilerParams(vmem_limit_bytes=VMEM_LIMIT)

    def sums(rows, dtype=jnp.bfloat16):
        return jax.ShapeDtypeStruct((rows, 128), dtype)

    place = pl.pallas_call(
        place_kernel,
        out_shape=jax.ShapeDtypeStruct((1, 128), jnp.int32),
        out_specs=vmem,
        compiler_params=pltpu.CompilerParams(vmem_limit_bytes=VMEM_LIMIT),
        cost_estimate=HEAD_COST,
    )()
    obs_count, place = lax.optimization_barrier((obs_count, place))
    terms, weights, far = pl.pallas_call(
        functools.partial(terms_kernel, sub_count, regions),
        out_shape=(
            jax.ShapeDtypeStruct((blocks, USED, 128), jnp.float32),
            jax.ShapeDtypeStruct((3 * sub_count, blocks, 128), jnp.float32),
            sums(wide),
        ),
        in_specs=[pl.BlockSpec(memory_space=pltpu.SMEM)] + [vmem] * 6,
        out_specs=(vmem,) * 3,
        scratch_shapes=[
            pltpu.VMEM((8, 128), jnp.float32),
            pltpu.VMEM((blocks, 128), jnp.float32),
            pltpu.VMEM((blocks, 128), jnp.float32),
        ],
        compiler_params=pltpu.CompilerParams(vmem_limit_bytes=VMEM_LIMIT),
        cost_estimate=pl.CostEstimate(flops=2 * blocks * 80 * 256 * 128, bytes_accessed=blocks * 64 * 128 * 2, transcendentals=0),
    )(obs_count, place, influence.T, taper_level.T, innovations, obs_error, obs_anom)
    state_anom, far = lax.optimization_barrier((state_anom, far))
    devices = [(r, s) for r in range(regions) for s in range(sub_count)]
    index = {device: i for i, device in enumerate(devices)}

    def moved(x, region_to, step=0):
        return lax.ppermute(x, AXES, [(index[r, s], index[region_to(r), s ^ step]) for r, s in devices])

    def sibling(r):
        return r ^ 1

    def across(r):
        return (r + 2 * (r % 2) - 1) % regions

    from_far = moved(far, across)
    near, far_later = pl.pallas_call(
        functools.partial(near_kernel, sub_count),
        out_shape=(sums(narrow), sums(wide)),
        in_specs=[vmem] * 2,
        out_specs=(vmem, vmem),
        compiler_params=params,
        cost_estimate=pl.CostEstimate(flops=blocks * wide * 256, bytes_accessed=blocks * USED * 512, transcendentals=0),
    )(terms, weights)
    from_near = moved(near, sibling)
    from_far_later = moved(far_later, lambda r: sibling(across(r)))
    here, beside, later = pl.pallas_call(
        functools.partial(rest_kernel, sub_count),
        out_shape=(sums(wide, jnp.float32), sums(wide + 8), sums(wide, jnp.float32)),
        in_specs=[vmem] * 2,
        out_specs=(vmem,) * 3,
        compiler_params=params,
        cost_estimate=pl.CostEstimate(flops=3 * blocks * wide * 256, bytes_accessed=blocks * USED * 512, transcendentals=0),
    )(terms, weights)
    sent = pl.pallas_call(
        functools.partial(join_kernel, half),
        out_shape=sums(wide),
        in_specs=[vmem] * 3,
        out_specs=vmem,
        scratch_shapes=[pltpu.VMEM((wide, 128), jnp.float32)],
        compiler_params=params,
        cost_estimate=pl.CostEstimate(flops=wide * 256, bytes_accessed=wide * 1024, transcendentals=0),
    )(from_near, here, from_far)
    got = moved(sent, sibling, 1)
    parts = (moved(beside, sibling), got, later, from_far_later)
    step, count = 2, half
    while step < sub_count:
        sent, kept = pl.pallas_call(
            functools.partial(fold_kernel, count),
            out_shape=(sums(sum_rows(count // 2, 8)), sums(sum_rows(count // 2, 2))),
            in_specs=[vmem] * len(parts),
            out_specs=(vmem, vmem),
            scratch_shapes=[pltpu.VMEM((sum_rows(count, 8), 128), jnp.float32)],
            compiler_params=params,
            cost_estimate=pl.CostEstimate(flops=count * 64 * 128, bytes_accessed=count * 64 * 1024, transcendentals=0),
        )(*parts)
        got = moved(sent, sibling, step)
        parts = (moved(kept, sibling), got)
        step, count = 2 * step, count // 2
    increment, variance_drop = pl.pallas_call(
        project_kernel,
        out_shape=(jax.ShapeDtypeStruct((2, cells), jnp.float32),) * 2,
        in_specs=[vmem] * 3,
        out_specs=(vmem, vmem),
        scratch_shapes=[pltpu.VMEM((sum_rows(1, 8), 128), jnp.float32)],
        compiler_params=pltpu.CompilerParams(vmem_limit_bytes=VMEM_LIMIT),
        cost_estimate=pl.CostEstimate(flops=2 * 144 * 128 * cells, bytes_accessed=col_blocks * 64 * cells * 2, transcendentals=0),
    )(*parts, state_anom.reshape(col_blocks * members, cells))
    return (increment, variance_drop)


def solution(mesh):
    return jax.shard_map(
        local,
        mesh=mesh,
        in_specs=(
            P(AXES, None, None),
            P(AXES, None, None),
            P(AXES, None),
            P(AXES, None),
            P(AXES, None),
            P(AXES, None),
            P("region"),
        ),
        out_specs=(P(AXES, None), P(AXES, None)),
        check_vma=False,
    )
```

```python
import functools

import jax
import jax.numpy as jnp
from jax import lax
from jax.experimental import pallas as pl
from jax.experimental.pallas import tpu as pltpu
from jax.sharding import PartitionSpec as P

AXES = ("region", "sub")
HALF = 32
USED = 40
HEAD_COST = pl.CostEstimate(flops=10**10, bytes_accessed=10**8, transcendentals=0)
VMEM_LIMIT = 8 * 1024 * 1024


def lane_patterns(rows):
    row = lax.broadcasted_iota(jnp.int32, (rows, 128), 0)
    lane = lax.broadcasted_iota(jnp.int32, (rows, 128), 1)
    return row, lane, lane % HALF, (lane // HALF) % 2 == 0


def pack_weights(infl_ref, level_ref, rows_ref, weights_ref, group_regions, sub_here, sub_count):
    blocks = infl_ref.shape[1]
    rows_ref[...] = jnp.zeros_like(rows_ref)
    rows_ref[0:4, 0:blocks] = infl_ref[...].astype(jnp.float32)
    rows_ref[4:8, 0:blocks] = 1.0 - 0.25 * level_ref[...].astype(jnp.float32)
    columns = rows_ref[...].T
    targets = [jnp.broadcast_to(columns[0:blocks, n : n + 1], (blocks, 128)) for n in range(4)]
    tapers = [jnp.broadcast_to(columns[0:blocks, 4 + n : 5 + n], (blocks, 128)) for n in range(4)]
    local = lax.broadcasted_iota(jnp.int32, (blocks, 128), 1) // 64
    for g, region in enumerate(group_regions):
        for k, slot in enumerate(slot_order(sub_count)):
            first = (region * sub_count + (sub_here ^ slot)) * 2
            wanted = (first + local).astype(jnp.float32)
            weight = jnp.zeros((blocks, 128), jnp.float32)
            for n in range(4):
                weight = weight + jnp.where(targets[n] == wanted, tapers[n], 0.0)
            weights_ref[g * sub_count + k] = weight


def slot_order(sub_count):
    bits = sub_count.bit_length() - 1
    return sorted(range(sub_count), key=lambda i: [(i >> b) & 1 for b in range(bits)])


def neighbours(regions):
    here = lax.axis_index("region")
    odd = here % 2
    far = (here + 2 * odd - 1 + regions) % regions
    near = here + 1 - 2 * odd
    return here, near, far


def place_kernel(out_ref):
    out_ref[...] = lax.broadcasted_iota(jnp.int32, (1, 128), 1)


def terms_kernel(sub_count, regions, count_ref, *refs):
    obs_ref, terms_ref, weights_ref, far_ref = refs[5:9]
    first_here = lax.axis_index("sub") * (obs_ref.shape[0] * obs_ref.shape[2])
    some = first_here < count_ref[0]

    @pl.when(some)
    def _():
        write_terms(sub_count, regions, count_ref, *refs)

    @pl.when(jnp.logical_not(some))
    def _():
        for ref in (terms_ref, weights_ref, far_ref):
            ref[...] = jnp.zeros_like(ref)


def write_terms(sub_count, regions, count_ref, place_ref, infl_ref, level_ref, innov_ref, error_ref, obs_ref,
                 terms_ref, weights_ref, far_ref, rows_ref, error32, innov32):
    blocks, members, per_block = obs_ref.shape
    here, near, far = neighbours(regions)
    sub_here = lax.axis_index("sub")
    divisor = members - 1.0
    error32[...] = error_ref[...].astype(jnp.float32)
    innov32[...] = innov_ref[...].astype(jnp.float32)
    pack_weights(infl_ref, level_ref, rows_ref, weights_ref, (far, near, here), sub_here, sub_count)
    row, lane, column, even = lane_patterns(HALF)
    from_top = jnp.where(even, row - column, column - row) <= 0
    diagonal = (row == column) & ~even
    row8 = lax.broadcasted_iota(jnp.int32, (8, 128), 0)
    place = place_ref[...]
    left = count_ref[0] - sub_here * (blocks * per_block)
    for first in range(0, blocks, 2):
        raws, twice, innovs = [], [], []
        for b in (first, first + 1):
            raw = obs_ref[b]
            values = raw.astype(jnp.float32)
            spread = jnp.sum(values * values, axis=0, keepdims=True) / divisor
            usable = jnp.where(place + b * per_block < left, 1.0 / (divisor * divisor), 0.0)
            factor = usable / (spread + error32[b : b + 1, :])
            scaled = (values * factor).astype(jnp.bfloat16)
            raws.append(raw)
            twice += [scaled, scaled]
            innovs.append(jnp.broadcast_to(innov32[b : b + 1, :], (8, 128)))
        rows = raws + [jnp.concatenate(innovs, axis=0).astype(jnp.bfloat16)]
        products = lax.dot_general(
            jnp.concatenate(rows, axis=0),
            jnp.concatenate(twice, axis=0),
            (((1,), (1,)), ((), ())),
            preferred_element_type=jnp.float32,
        )
        for i in range(2):
            product = products[:, i * 128 : (i + 1) * 128]
            top = product[2 * i * HALF : (2 * i + 1) * HALF]
            bottom = product[(2 * i + 1) * HALF : (2 * i + 2) * HALF]
            weight = divisor * product[4 * HALF + 8 * i : 4 * HALF + 8 * (i + 1)]
            corner = jnp.sum(jnp.where(diagonal, bottom, 0.0), axis=0, keepdims=True)
            terms_ref[first + i, 0:HALF, :] = jnp.where(from_top, top, bottom)
            terms_ref[first + i, HALF:USED, :] = jnp.where(row8 % 2 == 0, weight, corner)
    write_sums(weights_ref, terms_ref, sub_count // 2, sub_count // 2, far_ref)


def write_sums(weights_ref, terms_ref, first, count, out_ref):
    blocks = terms_ref.shape[0]
    pair = lax.broadcasted_iota(jnp.int32, (8, 128), 0) // 2
    matrices, extras = [], []
    group = min(4, count)
    for k in range(0, count, group):
        totals = [jnp.zeros((USED, 128), jnp.float32) for _ in range(group)]
        for b in range(blocks):
            term = terms_ref[b]
            for i in range(group):
                totals[i] = totals[i] + weights_ref[first + k + i, b : b + 1, :] * term
        matrices += [total[:HALF] for total in totals]
        extra = totals[group - 1][HALF:]
        for i in range(group - 1):
            extra = jnp.where(pair == i, totals[i][HALF:], extra)
        extras.append(extra)
    rest = out_ref.shape[0] - sum_rows(count, 8)
    if rest > 0:
        extras.append(jnp.zeros((rest, 128), jnp.float32))
    out_ref[...] = jnp.concatenate(matrices + extras, axis=0)[: out_ref.shape[0]].astype(out_ref.dtype)


def near_kernel(sub_count, terms_ref, weights_ref, near_ref, far_later_ref):
    write_sums(weights_ref, terms_ref, 0, sub_count // 2, far_later_ref)
    write_sums(weights_ref, terms_ref, sub_count + sub_count // 2, sub_count // 2, near_ref)


def rest_kernel(sub_count, terms_ref, weights_ref, here_ref, beside_ref, later_ref):
    half = sub_count // 2
    write_sums(weights_ref, terms_ref, 2 * sub_count + half, half, here_ref)
    write_sums(weights_ref, terms_ref, 2 * sub_count, half, beside_ref)
    write_sums(weights_ref, terms_ref, sub_count, half, later_ref)


def join_kernel(count, *refs):
    *sums, sent_ref, scratch = refs
    sent_ref[...] = jnp.concatenate(added(count, sums, scratch), axis=0).astype(sent_ref.dtype)


def added(count, refs, scratch):
    total = sum(padded(ref, count, scratch) for ref in refs)
    return total[: count * HALF], total[count * HALF :]


def sum_rows(count, multiple):
    return count * HALF + -(-2 * count // multiple) * multiple


def padded(ref, count, scratch):
    rows = sum_rows(count, 8)
    sums = ref[...].astype(jnp.float32)
    if sums.shape[0] >= rows:
        return sums[:rows]
    scratch[: sums.shape[0], :] = sums
    return scratch[:rows, :]


def fold_kernel(count, *refs):
    *sums, sent_ref, kept_ref, scratch = refs
    matrix, extra = added(count, sums, scratch)
    half = count // 2
    if half % 4:
        high = pltpu.roll(extra, 8 - 2 * half, 0)
        low = extra
    else:
        low, high = extra[: 2 * half], extra[2 * half :]
    going = matrix[half * HALF :]
    sent_ref[...] = jnp.concatenate([going, high], axis=0).astype(sent_ref.dtype)
    kept = jnp.concatenate([matrix[: half * HALF], low], axis=0)
    kept_ref[...] = kept[: kept_ref.shape[0]].astype(kept_ref.dtype)


def project_kernel(kept_ref, got_ref, state_ref, increment_ref, drop_ref, scratch):
    matrix, extra = added(1, (kept_ref, got_ref), scratch)
    row, lane, column, even = lane_patterns(HALF)
    first = lane < 64
    place = jnp.where(even, row - column, column - row)
    top = matrix * jnp.where(place < 0, 2.0, jnp.where(place == 0, jnp.where(even, 1.0, 2.0), 0.0))
    bottom = jnp.where(place > 0, 2.0 * matrix, jnp.where((place == 0) & ~even, extra[1:2], 0.0))
    row16, lane16, _, _ = lane_patterns(16)
    weights = jnp.broadcast_to(extra[0:1], (16, 128))
    weights = jnp.where(row16 == lane16 // 64, weights, 0.0)
    mixer = jnp.concatenate(
        [
            jnp.where(first, top, 0.0),
            jnp.where(first, bottom, 0.0),
            jnp.where(first, 0.0, top),
            jnp.where(first, 0.0, bottom),
            weights,
        ],
        axis=0,
    ).astype(jnp.bfloat16)
    width = 512
    for at in range(0, state_ref.shape[1], width):
        state = state_ref[:, at : at + width]
        projected = jnp.dot(mixer, state, preferred_element_type=jnp.float32)
        product = state.astype(jnp.float32) * projected[:128]
        increment_ref[:, at : at + width] = projected[128:130]
        drop_ref[0:1, at : at + width] = jnp.sum(product[:64], axis=0, keepdims=True)
        drop_ref[1:2, at : at + width] = jnp.sum(product[64:], axis=0, keepdims=True)


def local(state_anom, obs_anom, innovations, obs_error, influence, taper_level, obs_count):
    sub_count = lax.axis_size("sub")
    regions = lax.axis_size("region")
    col_blocks, members, cells = state_anom.shape
    blocks = obs_anom.shape[0]
    assert (col_blocks, members, obs_anom.shape[2]) == (2, 64, 128)
    assert regions % 2 == 0 and sub_count in (4, 16, 64)
    vmem = pl.BlockSpec(memory_space=pltpu.VMEM)
    half = sub_count // 2
    wide, narrow = sum_rows(half, 8), sum_rows(half, 2)
    params = pltpu.CompilerParams(vmem_limit_bytes=VMEM_LIMIT)

    def sums(rows, dtype=jnp.bfloat16):
        return jax.ShapeDtypeStruct((rows, 128), dtype)

    place = pl.pallas_call(
        place_kernel,
        out_shape=jax.ShapeDtypeStruct((1, 128), jnp.int32),
        out_specs=vmem,
        compiler_params=pltpu.CompilerParams(vmem_limit_bytes=VMEM_LIMIT),
        cost_estimate=HEAD_COST,
    )()
    obs_count, place = lax.optimization_barrier((obs_count, place))
    terms, weights, far = pl.pallas_call(
        functools.partial(terms_kernel, sub_count, regions),
        out_shape=(
            jax.ShapeDtypeStruct((blocks, USED, 128), jnp.float32),
            jax.ShapeDtypeStruct((3 * sub_count, blocks, 128), jnp.float32),
            sums(wide),
        ),
        in_specs=[pl.BlockSpec(memory_space=pltpu.SMEM)] + [vmem] * 6,
        out_specs=(vmem,) * 3,
        scratch_shapes=[
            pltpu.VMEM((8, 128), jnp.float32),
            pltpu.VMEM((blocks, 128), jnp.float32),
            pltpu.VMEM((blocks, 128), jnp.float32),
        ],
        compiler_params=pltpu.CompilerParams(vmem_limit_bytes=VMEM_LIMIT),
        cost_estimate=pl.CostEstimate(flops=2 * blocks * 80 * 256 * 128, bytes_accessed=blocks * 64 * 128 * 2, transcendentals=0),
    )(obs_count, place, influence.T, taper_level.T, innovations, obs_error, obs_anom)
    state_anom, far = lax.optimization_barrier((state_anom, far))
    devices = [(r, s) for r in range(regions) for s in range(sub_count)]
    index = {device: i for i, device in enumerate(devices)}

    def moved(x, region_to, step=0):
        return lax.ppermute(x, AXES, [(index[r, s], index[region_to(r), s ^ step]) for r, s in devices])

    def sibling(r):
        return r ^ 1

    def across(r):
        return (r + 2 * (r % 2) - 1) % regions

    from_far = moved(far, across)
    near, far_later = pl.pallas_call(
        functools.partial(near_kernel, sub_count),
        out_shape=(sums(narrow), sums(wide)),
        in_specs=[vmem] * 2,
        out_specs=(vmem, vmem),
        compiler_params=params,
        cost_estimate=pl.CostEstimate(flops=blocks * wide * 256, bytes_accessed=blocks * USED * 512, transcendentals=0),
    )(terms, weights)
    from_near = moved(near, sibling)
    from_far_later = moved(far_later, lambda r: sibling(across(r)))
    here, beside, later = pl.pallas_call(
        functools.partial(rest_kernel, sub_count),
        out_shape=(sums(wide, jnp.float32), sums(wide + 8), sums(wide, jnp.float32)),
        in_specs=[vmem] * 2,
        out_specs=(vmem,) * 3,
        compiler_params=params,
        cost_estimate=pl.CostEstimate(flops=3 * blocks * wide * 256, bytes_accessed=blocks * USED * 512, transcendentals=0),
    )(terms, weights)
    sent = pl.pallas_call(
        functools.partial(join_kernel, half),
        out_shape=sums(wide),
        in_specs=[vmem] * 3,
        out_specs=vmem,
        scratch_shapes=[pltpu.VMEM((wide, 128), jnp.float32)],
        compiler_params=params,
        cost_estimate=pl.CostEstimate(flops=wide * 256, bytes_accessed=wide * 1024, transcendentals=0),
    )(from_near, here, from_far)
    got = moved(sent, sibling, 1)
    parts = (moved(beside, sibling), got, later, from_far_later)
    step, count = 2, half
    while step < sub_count:
        sent, kept = pl.pallas_call(
            functools.partial(fold_kernel, count),
            out_shape=(sums(sum_rows(count // 2, 8)), sums(sum_rows(count // 2, 2))),
            in_specs=[vmem] * len(parts),
            out_specs=(vmem, vmem),
            scratch_shapes=[pltpu.VMEM((sum_rows(count, 8), 128), jnp.float32)],
            compiler_params=params,
            cost_estimate=pl.CostEstimate(flops=count * 64 * 128, bytes_accessed=count * 64 * 1024, transcendentals=0),
        )(*parts)
        got = moved(sent, sibling, step)
        parts = (moved(kept, sibling), got)
        step, count = 2 * step, count // 2
    increment, variance_drop = pl.pallas_call(
        project_kernel,
        out_shape=(jax.ShapeDtypeStruct((2, cells), jnp.float32),) * 2,
        in_specs=[vmem] * 3,
        out_specs=(vmem, vmem),
        scratch_shapes=[pltpu.VMEM((sum_rows(1, 8), 128), jnp.float32)],
        compiler_params=pltpu.CompilerParams(vmem_limit_bytes=VMEM_LIMIT),
        cost_estimate=pl.CostEstimate(flops=2 * 144 * 128 * cells, bytes_accessed=col_blocks * 64 * cells * 2, transcendentals=0),
    )(*parts, state_anom.reshape(col_blocks * members, cells))
    return (increment, variance_drop)


def solution(mesh):
    return jax.shard_map(
        local,
        mesh=mesh,
        in_specs=(
            P(AXES, None, None),
            P(AXES, None, None),
            P(AXES, None),
            P(AXES, None),
            P(AXES, None),
            P(AXES, None),
            P("region"),
        ),
        out_specs=(P(AXES, None), P(AXES, None)),
        check_vma=False,
    )
```

```python
import functools

import jax
import jax.numpy as jnp
from jax import lax
from jax.experimental import pallas as pl
from jax.experimental.pallas import tpu as pltpu
from jax.sharding import PartitionSpec as P

AXES = ("region", "sub")
HALF = 32
USED = 40
HEAD_COST = pl.CostEstimate(flops=10**10, bytes_accessed=10**8, transcendentals=0)
VMEM_LIMIT = 8 * 1024 * 1024


def lane_patterns(rows):
    row = lax.broadcasted_iota(jnp.int32, (rows, 128), 0)
    lane = lax.broadcasted_iota(jnp.int32, (rows, 128), 1)
    return row, lane, lane % HALF, (lane // HALF) % 2 == 0


def pack_weights(infl_ref, level_ref, rows_ref, weights_ref, group_regions, sub_here, sub_count):
    blocks = infl_ref.shape[1]
    rows_ref[...] = jnp.zeros_like(rows_ref)
    rows_ref[0:4, 0:blocks] = infl_ref[...].astype(jnp.float32)
    rows_ref[4:8, 0:blocks] = 1.0 - 0.25 * level_ref[...].astype(jnp.float32)
    columns = rows_ref[...].T
    targets = [jnp.broadcast_to(columns[0:blocks, n : n + 1], (blocks, 128)) for n in range(4)]
    tapers = [jnp.broadcast_to(columns[0:blocks, 4 + n : 5 + n], (blocks, 128)) for n in range(4)]
    local = lax.broadcasted_iota(jnp.int32, (blocks, 128), 1) // 64
    for g, region in enumerate(group_regions):
        for k, slot in enumerate(slot_order(sub_count)):
            first = (region * sub_count + (sub_here ^ slot)) * 2
            wanted = (first + local).astype(jnp.float32)
            weight = jnp.zeros((blocks, 128), jnp.float32)
            for n in range(4):
                weight = weight + jnp.where(targets[n] == wanted, tapers[n], 0.0)
            weights_ref[g * sub_count + k] = weight


def slot_order(sub_count):
    bits = sub_count.bit_length() - 1
    return sorted(range(sub_count), key=lambda i: [(i >> b) & 1 for b in range(bits)])


def neighbours(regions):
    here = lax.axis_index("region")
    odd = here % 2
    far = (here + 2 * odd - 1 + regions) % regions
    near = here + 1 - 2 * odd
    return here, near, far


def place_kernel(out_ref):
    out_ref[...] = lax.broadcasted_iota(jnp.int32, (1, 128), 1)


def terms_kernel(sub_count, regions, count_ref, *refs):
    obs_ref, terms_ref, weights_ref, far_ref = refs[5:9]
    first_here = lax.axis_index("sub") * (obs_ref.shape[0] * obs_ref.shape[2])
    some = first_here < count_ref[0]

    @pl.when(some)
    def _():
        write_terms(sub_count, regions, count_ref, *refs)

    @pl.when(jnp.logical_not(some))
    def _():
        for ref in (terms_ref, weights_ref, far_ref):
            ref[...] = jnp.zeros_like(ref)


def write_terms(sub_count, regions, count_ref, place_ref, infl_ref, level_ref, innov_ref, error_ref, obs_ref,
                 terms_ref, weights_ref, far_ref, rows_ref, error32, innov32):
    blocks, members, per_block = obs_ref.shape
    here, near, far = neighbours(regions)
    sub_here = lax.axis_index("sub")
    divisor = members - 1.0
    error32[...] = error_ref[...].astype(jnp.float32)
    innov32[...] = innov_ref[...].astype(jnp.float32)
    pack_weights(infl_ref, level_ref, rows_ref, weights_ref, (far, near, here), sub_here, sub_count)
    row, lane, column, even = lane_patterns(HALF)
    from_top = jnp.where(even, row - column, column - row) <= 0
    diagonal = (row == column) & ~even
    row8 = lax.broadcasted_iota(jnp.int32, (8, 128), 0)
    place = place_ref[...]
    left = count_ref[0] - sub_here * (blocks * per_block)
    for first in range(0, blocks, 2):
        raws, twice, innovs = [], [], []
        for b in (first, first + 1):
            raw = obs_ref[b]
            values = raw.astype(jnp.float32)
            spread = jnp.sum(values * values, axis=0, keepdims=True) / divisor
            usable = jnp.where(place + b * per_block < left, 1.0 / (divisor * divisor), 0.0)
            factor = usable / (spread + error32[b : b + 1, :])
            scaled = (values * factor).astype(jnp.bfloat16)
            raws.append(raw)
            twice += [scaled, scaled]
            innovs.append(jnp.broadcast_to(innov32[b : b + 1, :], (8, 128)))
        rows = raws + [jnp.concatenate(innovs, axis=0).astype(jnp.bfloat16)]
        products = lax.dot_general(
            jnp.concatenate(rows, axis=0),
            jnp.concatenate(twice, axis=0),
            (((1,), (1,)), ((), ())),
            preferred_element_type=jnp.float32,
        )
        for i in range(2):
            product = products[:, i * 128 : (i + 1) * 128]
            top = product[2 * i * HALF : (2 * i + 1) * HALF]
            bottom = product[(2 * i + 1) * HALF : (2 * i + 2) * HALF]
            weight = divisor * product[4 * HALF + 8 * i : 4 * HALF + 8 * (i + 1)]
            corner = jnp.sum(jnp.where(diagonal, bottom, 0.0), axis=0, keepdims=True)
            terms_ref[first + i, 0:HALF, :] = jnp.where(from_top, top, bottom)
            terms_ref[first + i, HALF:USED, :] = jnp.where(row8 % 2 == 0, weight, corner)
    write_sums(weights_ref, terms_ref, sub_count // 2, sub_count // 2, far_ref)


def write_sums(weights_ref, terms_ref, first, count, out_ref):
    blocks = terms_ref.shape[0]
    pair = lax.broadcasted_iota(jnp.int32, (8, 128), 0) // 2
    matrices, extras = [], []
    group = min(4, count)
    for k in range(0, count, group):
        totals = [jnp.zeros((USED, 128), jnp.float32) for _ in range(group)]
        for b in range(blocks):
            term = terms_ref[b]
            for i in range(group):
                totals[i] = totals[i] + weights_ref[first + k + i, b : b + 1, :] * term
        matrices += [total[:HALF] for total in totals]
        extra = totals[group - 1][HALF:]
        for i in range(group - 1):
            extra = jnp.where(pair == i, totals[i][HALF:], extra)
        extras.append(extra)
    rest = out_ref.shape[0] - sum_rows(count, 8)
    if rest > 0:
        extras.append(jnp.zeros((rest, 128), jnp.float32))
    out_ref[...] = jnp.concatenate(matrices + extras, axis=0)[: out_ref.shape[0]].astype(out_ref.dtype)


def near_kernel(sub_count, terms_ref, weights_ref, near_ref, far_later_ref):
    write_sums(weights_ref, terms_ref, 0, sub_count // 2, far_later_ref)
    write_sums(weights_ref, terms_ref, sub_count + sub_count // 2, sub_count // 2, near_ref)


def rest_kernel(sub_count, terms_ref, weights_ref, here_ref, beside_ref, later_ref):
    half = sub_count // 2
    write_sums(weights_ref, terms_ref, 2 * sub_count + half, half, here_ref)
    write_sums(weights_ref, terms_ref, 2 * sub_count, half, beside_ref)
    write_sums(weights_ref, terms_ref, sub_count, half, later_ref)


def join_kernel(count, *refs):
    *sums, sent_ref, scratch = refs
    sent_ref[...] = jnp.concatenate(added(count, sums, scratch), axis=0).astype(sent_ref.dtype)


def added(count, refs, scratch):
    total = sum(padded(ref, count, scratch) for ref in refs)
    return total[: count * HALF], total[count * HALF :]


def sum_rows(count, multiple):
    return count * HALF + -(-2 * count // multiple) * multiple


def padded(ref, count, scratch):
    rows = sum_rows(count, 8)
    sums = ref[...].astype(jnp.float32)
    if sums.shape[0] >= rows:
        return sums[:rows]
    scratch[: sums.shape[0], :] = sums
    return scratch[:rows, :]


def fold_kernel(count, *refs):
    *sums, sent_ref, kept_ref, scratch = refs
    matrix, extra = added(count, sums, scratch)
    half = count // 2
    if half % 4:
        high = pltpu.roll(extra, 8 - 2 * half, 0)
        low = extra
    else:
        low, high = extra[: 2 * half], extra[2 * half :]
    going = matrix[half * HALF :]
    sent_ref[...] = jnp.concatenate([going, high], axis=0).astype(sent_ref.dtype)
    kept = jnp.concatenate([matrix[: half * HALF], low], axis=0)
    kept_ref[...] = kept[: kept_ref.shape[0]].astype(kept_ref.dtype)


def project_kernel(kept_ref, got_ref, state_ref, increment_ref, drop_ref, scratch):
    matrix, extra = added(1, (kept_ref, got_ref), scratch)
    row, lane, column, even = lane_patterns(HALF)
    first = lane < 64
    place = jnp.where(even, row - column, column - row)
    top = matrix * jnp.where(place < 0, 2.0, jnp.where(place == 0, jnp.where(even, 1.0, 2.0), 0.0))
    bottom = jnp.where(place > 0, 2.0 * matrix, jnp.where((place == 0) & ~even, extra[1:2], 0.0))
    row16, lane16, _, _ = lane_patterns(16)
    weights = jnp.broadcast_to(extra[0:1], (16, 128))
    near = weights.astype(jnp.bfloat16).astype(jnp.float32)
    weights = jnp.where(row16 == lane16 // 64, near, jnp.where(row16 == lane16 // 64 + 2, weights - near, 0.0))
    mixer = jnp.concatenate(
        [
            jnp.where(first, top, 0.0),
            jnp.where(first, bottom, 0.0),
            jnp.where(first, 0.0, top),
            jnp.where(first, 0.0, bottom),
            weights,
        ],
        axis=0,
    ).astype(jnp.bfloat16)
    width = 512
    for at in range(0, state_ref.shape[1], width):
        state = state_ref[:, at : at + width]
        projected = jnp.dot(mixer, state, preferred_element_type=jnp.float32)
        product = state.astype(jnp.float32) * projected[:128]
        increment_ref[:, at : at + width] = projected[128:130] + projected[130:132]
        drop_ref[0:1, at : at + width] = jnp.sum(product[:64], axis=0, keepdims=True)
        drop_ref[1:2, at : at + width] = jnp.sum(product[64:], axis=0, keepdims=True)


def local(state_anom, obs_anom, innovations, obs_error, influence, taper_level, obs_count):
    sub_count = lax.axis_size("sub")
    regions = lax.axis_size("region")
    col_blocks, members, cells = state_anom.shape
    blocks = obs_anom.shape[0]
    assert (col_blocks, members, obs_anom.shape[2]) == (2, 64, 128)
    assert regions % 2 == 0 and sub_count in (4, 16, 64)
    vmem = pl.BlockSpec(memory_space=pltpu.VMEM)
    half = sub_count // 2
    wide, narrow = sum_rows(half, 8), sum_rows(half, 2)
    params = pltpu.CompilerParams(vmem_limit_bytes=VMEM_LIMIT)

    def sums(rows, dtype=jnp.bfloat16):
        return jax.ShapeDtypeStruct((rows, 128), dtype)

    place = pl.pallas_call(
        place_kernel,
        out_shape=jax.ShapeDtypeStruct((1, 128), jnp.int32),
        out_specs=vmem,
        compiler_params=pltpu.CompilerParams(vmem_limit_bytes=VMEM_LIMIT),
        cost_estimate=HEAD_COST,
    )()
    obs_count, place = lax.optimization_barrier((obs_count, place))
    terms, weights, far = pl.pallas_call(
        functools.partial(terms_kernel, sub_count, regions),
        out_shape=(
            jax.ShapeDtypeStruct((blocks, USED, 128), jnp.float32),
            jax.ShapeDtypeStruct((3 * sub_count, blocks, 128), jnp.float32),
            sums(wide),
        ),
        in_specs=[pl.BlockSpec(memory_space=pltpu.SMEM)] + [vmem] * 6,
        out_specs=(vmem,) * 3,
        scratch_shapes=[
            pltpu.VMEM((8, 128), jnp.float32),
            pltpu.VMEM((blocks, 128), jnp.float32),
            pltpu.VMEM((blocks, 128), jnp.float32),
        ],
        compiler_params=pltpu.CompilerParams(vmem_limit_bytes=VMEM_LIMIT),
        cost_estimate=pl.CostEstimate(flops=2 * blocks * 80 * 256 * 128, bytes_accessed=blocks * 64 * 128 * 2, transcendentals=0),
    )(obs_count, place, influence.T, taper_level.T, innovations, obs_error, obs_anom)
    state_anom, far = lax.optimization_barrier((state_anom, far))
    devices = [(r, s) for r in range(regions) for s in range(sub_count)]
    index = {device: i for i, device in enumerate(devices)}

    def moved(x, region_to, step=0):
        return lax.ppermute(x, AXES, [(index[r, s], index[region_to(r), s ^ step]) for r, s in devices])

    def sibling(r):
        return r ^ 1

    def across(r):
        return (r + 2 * (r % 2) - 1) % regions

    from_far = moved(far, across)
    near, far_later = pl.pallas_call(
        functools.partial(near_kernel, sub_count),
        out_shape=(sums(narrow), sums(wide)),
        in_specs=[vmem] * 2,
        out_specs=(vmem, vmem),
        compiler_params=params,
        cost_estimate=pl.CostEstimate(flops=blocks * wide * 256, bytes_accessed=blocks * USED * 512, transcendentals=0),
    )(terms, weights)
    from_near = moved(near, sibling)
    from_far_later = moved(far_later, lambda r: sibling(across(r)))
    here, beside, later = pl.pallas_call(
        functools.partial(rest_kernel, sub_count),
        out_shape=(sums(wide, jnp.float32), sums(wide + 8), sums(wide, jnp.float32)),
        in_specs=[vmem] * 2,
        out_specs=(vmem,) * 3,
        compiler_params=params,
        cost_estimate=pl.CostEstimate(flops=3 * blocks * wide * 256, bytes_accessed=blocks * USED * 512, transcendentals=0),
    )(terms, weights)
    sent = pl.pallas_call(
        functools.partial(join_kernel, half),
        out_shape=sums(wide),
        in_specs=[vmem] * 3,
        out_specs=vmem,
        scratch_shapes=[pltpu.VMEM((wide, 128), jnp.float32)],
        compiler_params=params,
        cost_estimate=pl.CostEstimate(flops=wide * 256, bytes_accessed=wide * 1024, transcendentals=0),
    )(from_near, here, from_far)
    got = moved(sent, sibling, 1)
    parts = (moved(beside, sibling), got, later, from_far_later)
    step, count = 2, half
    while step < sub_count:
        sent, kept = pl.pallas_call(
            functools.partial(fold_kernel, count),
            out_shape=(sums(sum_rows(count // 2, 8)), sums(sum_rows(count // 2, 2))),
            in_specs=[vmem] * len(parts),
            out_specs=(vmem, vmem),
            scratch_shapes=[pltpu.VMEM((sum_rows(count, 8), 128), jnp.float32)],
            compiler_params=params,
            cost_estimate=pl.CostEstimate(flops=count * 64 * 128, bytes_accessed=count * 64 * 1024, transcendentals=0),
        )(*parts)
        got = moved(sent, sibling, step)
        parts = (moved(kept, sibling), got)
        step, count = 2 * step, count // 2
    increment, variance_drop = pl.pallas_call(
        project_kernel,
        out_shape=(jax.ShapeDtypeStruct((2, cells), jnp.float32),) * 2,
        in_specs=[vmem] * 3,
        out_specs=(vmem, vmem),
        scratch_shapes=[pltpu.VMEM((sum_rows(1, 8), 128), jnp.float32)],
        compiler_params=pltpu.CompilerParams(vmem_limit_bytes=VMEM_LIMIT),
        cost_estimate=pl.CostEstimate(flops=2 * 144 * 128 * cells, bytes_accessed=col_blocks * 64 * cells * 2, transcendentals=0),
    )(*parts, state_anom.reshape(col_blocks * members, cells))
    return (increment, variance_drop)


def solution(mesh):
    return jax.shard_map(
        local,
        mesh=mesh,
        in_specs=(
            P(AXES, None, None),
            P(AXES, None, None),
            P(AXES, None),
            P(AXES, None),
            P(AXES, None),
            P(AXES, None),
            P("region"),
        ),
        out_specs=(P(AXES, None), P(AXES, None)),
        check_vma=False,
    )
```

```python
import functools

import jax
import jax.numpy as jnp
from jax import lax
from jax.experimental import pallas as pl
from jax.experimental.pallas import tpu as pltpu
from jax.sharding import PartitionSpec as P

AXES = ("region", "sub")
HALF = 32
USED = 40
HEAD_COST = pl.CostEstimate(flops=10**10, bytes_accessed=10**8, transcendentals=0)
VMEM_LIMIT = 8 * 1024 * 1024


def lane_patterns(rows):
    row = lax.broadcasted_iota(jnp.int32, (rows, 128), 0)
    lane = lax.broadcasted_iota(jnp.int32, (rows, 128), 1)
    return row, lane, lane % HALF, (lane // HALF) % 2 == 0


def pack_weights(infl_ref, level_ref, rows_ref, weights_ref, group_regions, sub_here, sub_count):
    blocks = infl_ref.shape[1]
    rows_ref[...] = jnp.zeros_like(rows_ref)
    rows_ref[0:4, 0:blocks] = infl_ref[...].astype(jnp.float32)
    rows_ref[4:8, 0:blocks] = 1.0 - 0.25 * level_ref[...].astype(jnp.float32)
    columns = rows_ref[...].T
    targets = [jnp.broadcast_to(columns[0:blocks, n : n + 1], (blocks, 128)) for n in range(4)]
    tapers = [jnp.broadcast_to(columns[0:blocks, 4 + n : 5 + n], (blocks, 128)) for n in range(4)]
    local = lax.broadcasted_iota(jnp.int32, (blocks, 128), 1) // 64
    for g, region in enumerate(group_regions):
        for k, slot in enumerate(slot_order(sub_count)):
            first = (region * sub_count + (sub_here ^ slot)) * 2
            wanted = (first + local).astype(jnp.float32)
            weight = jnp.zeros((blocks, 128), jnp.float32)
            for n in range(4):
                weight = weight + jnp.where(targets[n] == wanted, tapers[n], 0.0)
            weights_ref[g * sub_count + k] = weight


def slot_order(sub_count):
    bits = sub_count.bit_length() - 1
    return sorted(range(sub_count), key=lambda i: [(i >> b) & 1 for b in range(bits)])


def neighbours(regions):
    here = lax.axis_index("region")
    odd = here % 2
    far = (here + 2 * odd - 1 + regions) % regions
    near = here + 1 - 2 * odd
    return here, near, far


def place_kernel(out_ref):
    out_ref[...] = lax.broadcasted_iota(jnp.int32, (1, 128), 1)


def terms_kernel(sub_count, regions, count_ref, *refs):
    obs_ref, terms_ref, weights_ref, far_ref = refs[5:9]
    first_here = lax.axis_index("sub") * (obs_ref.shape[0] * obs_ref.shape[2])
    some = first_here < count_ref[0]

    @pl.when(some)
    def _():
        write_terms(sub_count, regions, count_ref, *refs)

    @pl.when(jnp.logical_not(some))
    def _():
        for ref in (terms_ref, weights_ref, far_ref):
            ref[...] = jnp.zeros_like(ref)


def write_terms(sub_count, regions, count_ref, place_ref, infl_ref, level_ref, innov_ref, error_ref, obs_ref,
                 terms_ref, weights_ref, far_ref, rows_ref, error32, innov32):
    blocks, members, per_block = obs_ref.shape
    here, near, far = neighbours(regions)
    sub_here = lax.axis_index("sub")
    divisor = members - 1.0
    error32[...] = error_ref[...].astype(jnp.float32)
    innov32[...] = innov_ref[...].astype(jnp.float32)
    pack_weights(infl_ref, level_ref, rows_ref, weights_ref, (far, near, here), sub_here, sub_count)
    row, lane, column, even = lane_patterns(HALF)
    from_top = jnp.where(even, row - column, column - row) <= 0
    diagonal = (row == column) & ~even
    row8 = lax.broadcasted_iota(jnp.int32, (8, 128), 0)
    place = place_ref[...]
    left = count_ref[0] - sub_here * (blocks * per_block)
    for first in range(0, blocks, 2):
        raws, twice, innovs = [], [], []
        for b in (first, first + 1):
            raw = obs_ref[b]
            values = raw.astype(jnp.float32)
            spread = jnp.sum(values * values, axis=0, keepdims=True) / divisor
            usable = jnp.where(place + b * per_block < left, 1.0 / (divisor * divisor), 0.0)
            factor = usable / (spread + error32[b : b + 1, :])
            scaled = (values * factor).astype(jnp.bfloat16)
            raws.append(raw)
            twice += [scaled, scaled]
            innovs.append(jnp.broadcast_to(innov32[b : b + 1, :], (8, 128)))
        rows = raws + [jnp.concatenate(innovs, axis=0).astype(jnp.bfloat16)]
        products = lax.dot_general(
            jnp.concatenate(rows, axis=0),
            jnp.concatenate(twice, axis=0),
            (((1,), (1,)), ((), ())),
            preferred_element_type=jnp.float32,
        )
        for i in range(2):
            product = products[:, i * 128 : (i + 1) * 128]
            top = product[2 * i * HALF : (2 * i + 1) * HALF]
            bottom = product[(2 * i + 1) * HALF : (2 * i + 2) * HALF]
            weight = divisor * product[4 * HALF + 8 * i : 4 * HALF + 8 * (i + 1)]
            corner = jnp.sum(jnp.where(diagonal, bottom, 0.0), axis=0, keepdims=True)
            terms_ref[first + i, 0:HALF, :] = jnp.where(from_top, top, bottom)
            terms_ref[first + i, HALF:USED, :] = jnp.where(row8 % 2 == 0, weight, corner)
    write_sums(weights_ref, terms_ref, sub_count // 2, sub_count // 2, far_ref)


def write_sums(weights_ref, terms_ref, first, count, out_ref):
    blocks = terms_ref.shape[0]
    pair = lax.broadcasted_iota(jnp.int32, (8, 128), 0) // 2
    matrices, extras = [], []
    group = min(4, count)
    for k in range(0, count, group):
        totals = [jnp.zeros((USED, 128), jnp.float32) for _ in range(group)]
        for b in range(blocks):
            term = terms_ref[b]
            for i in range(group):
                totals[i] = totals[i] + weights_ref[first + k + i, b : b + 1, :] * term
        matrices += [total[:HALF] for total in totals]
        extra = totals[group - 1][HALF:]
        for i in range(group - 1):
            extra = jnp.where(pair == i, totals[i][HALF:], extra)
        extras.append(extra)
    rest = out_ref.shape[0] - sum_rows(count, 8)
    if rest > 0:
        extras.append(jnp.zeros((rest, 128), jnp.float32))
    out_ref[...] = jnp.concatenate(matrices + extras, axis=0)[: out_ref.shape[0]].astype(out_ref.dtype)


def unless_empty(make, count_ref, terms_ref, out_refs):
    some = lax.axis_index("sub") * (terms_ref.shape[0] * 128) < count_ref[0]
    pl.when(some)(make)

    @pl.when(jnp.logical_not(some))
    def _():
        for ref in out_refs:
            ref[...] = jnp.zeros_like(ref)


def near_kernel(sub_count, count_ref, terms_ref, weights_ref, *out_refs):
    unless_empty(lambda: near_sums(sub_count, terms_ref, weights_ref, *out_refs), count_ref, terms_ref, out_refs)


def rest_kernel(sub_count, count_ref, terms_ref, weights_ref, *out_refs):
    unless_empty(lambda: rest_sums(sub_count, terms_ref, weights_ref, *out_refs), count_ref, terms_ref, out_refs)


def near_sums(sub_count, terms_ref, weights_ref, near_ref, far_later_ref):
    write_sums(weights_ref, terms_ref, 0, sub_count // 2, far_later_ref)
    write_sums(weights_ref, terms_ref, sub_count + sub_count // 2, sub_count // 2, near_ref)


def rest_sums(sub_count, terms_ref, weights_ref, here_ref, beside_ref, later_ref):
    half = sub_count // 2
    write_sums(weights_ref, terms_ref, 2 * sub_count + half, half, here_ref)
    write_sums(weights_ref, terms_ref, 2 * sub_count, half, beside_ref)
    write_sums(weights_ref, terms_ref, sub_count, half, later_ref)


def join_kernel(count, *refs):
    *sums, sent_ref, scratch = refs
    sent_ref[...] = jnp.concatenate(added(count, sums, scratch), axis=0).astype(sent_ref.dtype)


def added(count, refs, scratch):
    total = sum(padded(ref, count, scratch) for ref in refs)
    return total[: count * HALF], total[count * HALF :]


def sum_rows(count, multiple):
    return count * HALF + -(-2 * count // multiple) * multiple


def padded(ref, count, scratch):
    rows = sum_rows(count, 8)
    sums = ref[...].astype(jnp.float32)
    if sums.shape[0] >= rows:
        return sums[:rows]
    scratch[: sums.shape[0], :] = sums
    return scratch[:rows, :]


def fold_kernel(count, *refs):
    *sums, sent_ref, kept_ref, scratch = refs
    matrix, extra = added(count, sums, scratch)
    half = count // 2
    if half % 4:
        high = pltpu.roll(extra, 8 - 2 * half, 0)
        low = extra
    else:
        low, high = extra[: 2 * half], extra[2 * half :]
    going = matrix[half * HALF :]
    sent_ref[...] = jnp.concatenate([going, high], axis=0).astype(sent_ref.dtype)
    kept = jnp.concatenate([matrix[: half * HALF], low], axis=0)
    kept_ref[...] = kept[: kept_ref.shape[0]].astype(kept_ref.dtype)


def project_kernel(kept_ref, got_ref, state_ref, increment_ref, drop_ref, scratch):
    matrix, extra = added(1, (kept_ref, got_ref), scratch)
    row, lane, column, even = lane_patterns(HALF)
    first = lane < 64
    place = jnp.where(even, row - column, column - row)
    top = matrix * jnp.where(place < 0, 2.0, jnp.where(place == 0, jnp.where(even, 1.0, 2.0), 0.0))
    bottom = jnp.where(place > 0, 2.0 * matrix, jnp.where((place == 0) & ~even, extra[1:2], 0.0))
    row16, lane16, _, _ = lane_patterns(16)
    weights = jnp.broadcast_to(extra[0:1], (16, 128))
    weights = jnp.where(row16 == lane16 // 64, weights, 0.0)
    mixer = jnp.concatenate(
        [
            jnp.where(first, top, 0.0),
            jnp.where(first, bottom, 0.0),
            jnp.where(first, 0.0, top),
            jnp.where(first, 0.0, bottom),
            weights,
        ],
        axis=0,
    ).astype(jnp.bfloat16)
    width = 512
    for at in range(0, state_ref.shape[1], width):
        state = state_ref[:, at : at + width]
        projected = jnp.dot(mixer, state, preferred_element_type=jnp.float32)
        product = state.astype(jnp.float32) * projected[:128]
        increment_ref[:, at : at + width] = projected[128:130]
        drop_ref[0:1, at : at + width] = jnp.sum(product[:64], axis=0, keepdims=True)
        drop_ref[1:2, at : at + width] = jnp.sum(product[64:], axis=0, keepdims=True)


def local(state_anom, obs_anom, innovations, obs_error, influence, taper_level, obs_count):
    sub_count = lax.axis_size("sub")
    regions = lax.axis_size("region")
    col_blocks, members, cells = state_anom.shape
    blocks = obs_anom.shape[0]
    assert (col_blocks, members, obs_anom.shape[2]) == (2, 64, 128)
    assert regions % 2 == 0 and sub_count in (4, 16, 64)
    vmem = pl.BlockSpec(memory_space=pltpu.VMEM)
    half = sub_count // 2
    wide, narrow = sum_rows(half, 8), sum_rows(half, 2)
    params = pltpu.CompilerParams(vmem_limit_bytes=VMEM_LIMIT)

    def sums(rows, dtype=jnp.bfloat16):
        return jax.ShapeDtypeStruct((rows, 128), dtype)

    place = pl.pallas_call(
        place_kernel,
        out_shape=jax.ShapeDtypeStruct((1, 128), jnp.int32),
        out_specs=vmem,
        compiler_params=pltpu.CompilerParams(vmem_limit_bytes=VMEM_LIMIT),
        cost_estimate=HEAD_COST,
    )()
    obs_count, place = lax.optimization_barrier((obs_count, place))
    terms, weights, far = pl.pallas_call(
        functools.partial(terms_kernel, sub_count, regions),
        out_shape=(
            jax.ShapeDtypeStruct((blocks, USED, 128), jnp.float32),
            jax.ShapeDtypeStruct((3 * sub_count, blocks, 128), jnp.float32),
            sums(wide),
        ),
        in_specs=[pl.BlockSpec(memory_space=pltpu.SMEM)] + [vmem] * 6,
        out_specs=(vmem,) * 3,
        scratch_shapes=[
            pltpu.VMEM((8, 128), jnp.float32),
            pltpu.VMEM((blocks, 128), jnp.float32),
            pltpu.VMEM((blocks, 128), jnp.float32),
        ],
        compiler_params=pltpu.CompilerParams(vmem_limit_bytes=VMEM_LIMIT),
        cost_estimate=pl.CostEstimate(flops=2 * blocks * 80 * 256 * 128, bytes_accessed=blocks * 64 * 128 * 2, transcendentals=0),
    )(obs_count, place, influence.T, taper_level.T, innovations, obs_error, obs_anom)
    state_anom, far = lax.optimization_barrier((state_anom, far))
    devices = [(r, s) for r in range(regions) for s in range(sub_count)]
    index = {device: i for i, device in enumerate(devices)}

    def moved(x, region_to, step=0):
        return lax.ppermute(x, AXES, [(index[r, s], index[region_to(r), s ^ step]) for r, s in devices])

    def sibling(r):
        return r ^ 1

    def across(r):
        return (r + 2 * (r % 2) - 1) % regions

    from_far = moved(far, across)
    near, far_later = pl.pallas_call(
        functools.partial(near_kernel, sub_count),
        out_shape=(sums(narrow), sums(wide)),
        in_specs=[pl.BlockSpec(memory_space=pltpu.SMEM)] + [vmem] * 2,
        out_specs=(vmem, vmem),
        compiler_params=params,
        cost_estimate=pl.CostEstimate(flops=blocks * wide * 256, bytes_accessed=blocks * USED * 512, transcendentals=0),
    )(obs_count, terms, weights)
    from_near = moved(near, sibling)
    from_far_later = moved(far_later, lambda r: sibling(across(r)))
    here, beside, later = pl.pallas_call(
        functools.partial(rest_kernel, sub_count),
        out_shape=(sums(wide, jnp.float32), sums(wide + 8), sums(wide, jnp.float32)),
        in_specs=[pl.BlockSpec(memory_space=pltpu.SMEM)] + [vmem] * 2,
        out_specs=(vmem,) * 3,
        compiler_params=params,
        cost_estimate=pl.CostEstimate(flops=3 * blocks * wide * 256, bytes_accessed=blocks * USED * 512, transcendentals=0),
    )(obs_count, terms, weights)
    sent = pl.pallas_call(
        functools.partial(join_kernel, half),
        out_shape=sums(wide),
        in_specs=[vmem] * 3,
        out_specs=vmem,
        scratch_shapes=[pltpu.VMEM((wide, 128), jnp.float32)],
        compiler_params=params,
        cost_estimate=pl.CostEstimate(flops=wide * 256, bytes_accessed=wide * 1024, transcendentals=0),
    )(from_near, here, from_far)
    got = moved(sent, sibling, 1)
    parts = (moved(beside, sibling), got, later, from_far_later)
    step, count = 2, half
    while step < sub_count:
        sent, kept = pl.pallas_call(
            functools.partial(fold_kernel, count),
            out_shape=(sums(sum_rows(count // 2, 8)), sums(sum_rows(count // 2, 2))),
            in_specs=[vmem] * len(parts),
            out_specs=(vmem, vmem),
            scratch_shapes=[pltpu.VMEM((sum_rows(count, 8), 128), jnp.float32)],
            compiler_params=params,
            cost_estimate=pl.CostEstimate(flops=count * 64 * 128, bytes_accessed=count * 64 * 1024, transcendentals=0),
        )(*parts)
        got = moved(sent, sibling, step)
        parts = (moved(kept, sibling), got)
        step, count = 2 * step, count // 2
    increment, variance_drop = pl.pallas_call(
        project_kernel,
        out_shape=(jax.ShapeDtypeStruct((2, cells), jnp.float32),) * 2,
        in_specs=[vmem] * 3,
        out_specs=(vmem, vmem),
        scratch_shapes=[pltpu.VMEM((sum_rows(1, 8), 128), jnp.float32)],
        compiler_params=pltpu.CompilerParams(vmem_limit_bytes=VMEM_LIMIT),
        cost_estimate=pl.CostEstimate(flops=2 * 144 * 128 * cells, bytes_accessed=col_blocks * 64 * cells * 2, transcendentals=0),
    )(*parts, state_anom.reshape(col_blocks * members, cells))
    return (increment, variance_drop)


def solution(mesh):
    return jax.shard_map(
        local,
        mesh=mesh,
        in_specs=(
            P(AXES, None, None),
            P(AXES, None, None),
            P(AXES, None),
            P(AXES, None),
            P(AXES, None),
            P(AXES, None),
            P("region"),
        ),
        out_specs=(P(AXES, None), P(AXES, None)),
        check_vma=False,
    )
```

```python
import functools

import jax
import jax.numpy as jnp
from jax import lax
from jax.experimental import pallas as pl
from jax.experimental.pallas import tpu as pltpu
from jax.sharding import PartitionSpec as P

AXES = ("region", "sub")
HALF = 32
USED = 40
HEAD_COST = pl.CostEstimate(flops=10**10, bytes_accessed=10**8, transcendentals=0)
VMEM_LIMIT = 8 * 1024 * 1024


def lane_patterns(rows):
    row = lax.broadcasted_iota(jnp.int32, (rows, 128), 0)
    lane = lax.broadcasted_iota(jnp.int32, (rows, 128), 1)
    return row, lane, lane % HALF, (lane // HALF) % 2 == 0


def pack_weights(infl_ref, level_ref, rows_ref, weights_ref, group_regions, sub_here, sub_count):
    blocks = infl_ref.shape[1]
    rows_ref[...] = jnp.zeros_like(rows_ref)
    rows_ref[0:4, 0:blocks] = infl_ref[...].astype(jnp.float32)
    rows_ref[4:8, 0:blocks] = 1.0 - 0.25 * level_ref[...].astype(jnp.float32)
    columns = rows_ref[...].T
    targets = [jnp.broadcast_to(columns[0:blocks, n : n + 1], (blocks, 128)) for n in range(4)]
    tapers = [jnp.broadcast_to(columns[0:blocks, 4 + n : 5 + n], (blocks, 128)) for n in range(4)]
    local = lax.broadcasted_iota(jnp.int32, (blocks, 128), 1) // 64
    for g, region in enumerate(group_regions):
        for k, slot in enumerate(slot_order(sub_count)):
            first = (region * sub_count + (sub_here ^ slot)) * 2
            wanted = (first + local).astype(jnp.float32)
            weight = jnp.zeros((blocks, 128), jnp.float32)
            for n in range(4):
                weight = weight + jnp.where(targets[n] == wanted, tapers[n], 0.0)
            weights_ref[g * sub_count + k] = weight


def slot_order(sub_count):
    bits = sub_count.bit_length() - 1
    return sorted(range(sub_count), key=lambda i: [(i >> b) & 1 for b in range(bits)])


def neighbours(regions):
    here = lax.axis_index("region")
    odd = here % 2
    far = (here + 2 * odd - 1 + regions) % regions
    near = here + 1 - 2 * odd
    return here, near, far


def place_kernel(out_ref):
    out_ref[...] = lax.broadcasted_iota(jnp.int32, (1, 128), 1)


def terms_kernel(sub_count, regions, count_ref, *refs):
    obs_ref, terms_ref, weights_ref, far_ref = refs[5:9]
    first_here = lax.axis_index("sub") * (obs_ref.shape[0] * obs_ref.shape[2])
    some = first_here < count_ref[0]

    @pl.when(some)
    def _():
        write_terms(sub_count, regions, count_ref, *refs)

    @pl.when(jnp.logical_not(some))
    def _():
        for ref in (terms_ref, weights_ref, far_ref):
            ref[...] = jnp.zeros_like(ref)


def write_terms(sub_count, regions, count_ref, place_ref, infl_ref, level_ref, innov_ref, error_ref, obs_ref,
                 terms_ref, weights_ref, far_ref, rows_ref, error32, innov32):
    blocks, members, per_block = obs_ref.shape
    here, near, far = neighbours(regions)
    sub_here = lax.axis_index("sub")
    divisor = members - 1.0
    error32[...] = error_ref[...].astype(jnp.float32)
    innov32[...] = innov_ref[...].astype(jnp.float32)
    pack_weights(infl_ref, level_ref, rows_ref, weights_ref, (far, near, here), sub_here, sub_count)
    row, lane, column, even = lane_patterns(HALF)
    from_top = jnp.where(even, row - column, column - row) <= 0
    diagonal = (row == column) & ~even
    row8 = lax.broadcasted_iota(jnp.int32, (8, 128), 0)
    place = place_ref[...]
    left = count_ref[0] - sub_here * (blocks * per_block)
    for first in range(0, blocks, 2):
        raws, twice, innovs = [], [], []
        for b in (first, first + 1):
            raw = obs_ref[b]
            values = raw.astype(jnp.float32)
            spread = jnp.sum(values * values, axis=0, keepdims=True) / divisor
            usable = jnp.where(place + b * per_block < left, 1.0 / (divisor * divisor), 0.0)
            factor = usable / (spread + error32[b : b + 1, :])
            scaled = (values * factor).astype(jnp.bfloat16)
            raws.append(raw)
            twice += [scaled, scaled]
            innovs.append(innov32[b : b + 1, :])
        rows = raws + [jnp.where(row8 < 4, *innovs).astype(jnp.bfloat16)]
        products = lax.dot_general(
            jnp.concatenate(rows, axis=0),
            jnp.concatenate(twice, axis=0),
            (((1,), (1,)), ((), ())),
            preferred_element_type=jnp.float32,
        )
        for i in range(2):
            product = products[:, i * 128 : (i + 1) * 128]
            top = product[2 * i * HALF : (2 * i + 1) * HALF]
            bottom = product[(2 * i + 1) * HALF : (2 * i + 2) * HALF]
            weight = divisor * product[4 * HALF + 4 * i : 4 * HALF + 4 * i + 1]
            corner = jnp.sum(jnp.where(diagonal, bottom, 0.0), axis=0, keepdims=True)
            terms_ref[first + i, 0:HALF, :] = jnp.where(from_top, top, bottom)
            terms_ref[first + i, HALF:USED, :] = jnp.where(row8 % 2 == 0, weight, corner)
    write_sums(weights_ref, terms_ref, sub_count // 2, sub_count // 2, far_ref)


def write_sums(weights_ref, terms_ref, first, count, out_ref):
    blocks = terms_ref.shape[0]
    pair = lax.broadcasted_iota(jnp.int32, (8, 128), 0) // 2
    matrices, extras = [], []
    group = min(4, count)
    for k in range(0, count, group):
        totals = [jnp.zeros((USED, 128), jnp.float32) for _ in range(group)]
        for b in range(blocks):
            term = terms_ref[b]
            for i in range(group):
                totals[i] = totals[i] + weights_ref[first + k + i, b : b + 1, :] * term
        matrices += [total[:HALF] for total in totals]
        extra = totals[group - 1][HALF:]
        for i in range(group - 1):
            extra = jnp.where(pair == i, totals[i][HALF:], extra)
        extras.append(extra)
    rest = out_ref.shape[0] - sum_rows(count, 8)
    if rest > 0:
        extras.append(jnp.zeros((rest, 128), jnp.float32))
    out_ref[...] = jnp.concatenate(matrices + extras, axis=0)[: out_ref.shape[0]].astype(out_ref.dtype)


def near_kernel(sub_count, terms_ref, weights_ref, near_ref, far_later_ref):
    write_sums(weights_ref, terms_ref, 0, sub_count // 2, far_later_ref)
    write_sums(weights_ref, terms_ref, sub_count + sub_count // 2, sub_count // 2, near_ref)


def rest_kernel(sub_count, terms_ref, weights_ref, here_ref, beside_ref, later_ref):
    half = sub_count // 2
    write_sums(weights_ref, terms_ref, 2 * sub_count + half, half, here_ref)
    write_sums(weights_ref, terms_ref, 2 * sub_count, half, beside_ref)
    write_sums(weights_ref, terms_ref, sub_count, half, later_ref)


def join_kernel(count, *refs):
    *sums, sent_ref, scratch = refs
    sent_ref[...] = jnp.concatenate(added(count, sums, scratch), axis=0).astype(sent_ref.dtype)


def added(count, refs, scratch):
    total = sum(padded(ref, count, scratch) for ref in refs)
    return total[: count * HALF], total[count * HALF :]


def sum_rows(count, multiple):
    return count * HALF + -(-2 * count // multiple) * multiple


def padded(ref, count, scratch):
    rows = sum_rows(count, 8)
    sums = ref[...].astype(jnp.float32)
    if sums.shape[0] >= rows:
        return sums[:rows]
    scratch[: sums.shape[0], :] = sums
    return scratch[:rows, :]


def fold_kernel(count, *refs):
    *sums, sent_ref, kept_ref, scratch = refs
    matrix, extra = added(count, sums, scratch)
    half = count // 2
    if half % 4:
        high = pltpu.roll(extra, 8 - 2 * half, 0)
        low = extra
    else:
        low, high = extra[: 2 * half], extra[2 * half :]
    going = matrix[half * HALF :]
    sent_ref[...] = jnp.concatenate([going, high], axis=0).astype(sent_ref.dtype)
    kept = jnp.concatenate([matrix[: half * HALF], low], axis=0)
    kept_ref[...] = kept[: kept_ref.shape[0]].astype(kept_ref.dtype)


def project_kernel(kept_ref, got_ref, state_ref, increment_ref, drop_ref, scratch):
    matrix, extra = added(1, (kept_ref, got_ref), scratch)
    row, lane, column, even = lane_patterns(HALF)
    first = lane < 64
    place = jnp.where(even, row - column, column - row)
    top = matrix * jnp.where(place < 0, 2.0, jnp.where(place == 0, jnp.where(even, 1.0, 2.0), 0.0))
    bottom = jnp.where(place > 0, 2.0 * matrix, jnp.where((place == 0) & ~even, extra[1:2], 0.0))
    row16, lane16, _, _ = lane_patterns(16)
    weights = jnp.broadcast_to(extra[0:1], (16, 128))
    weights = jnp.where(row16 == lane16 // 64, weights, 0.0)
    mixer = jnp.concatenate(
        [
            jnp.where(first, top, 0.0),
            jnp.where(first, bottom, 0.0),
            jnp.where(first, 0.0, top),
            jnp.where(first, 0.0, bottom),
            weights,
        ],
        axis=0,
    ).astype(jnp.bfloat16)
    width = 512
    for at in range(0, state_ref.shape[1], width):
        state = state_ref[:, at : at + width]
        projected = jnp.dot(mixer, state, preferred_element_type=jnp.float32)
        product = state.astype(jnp.float32) * projected[:128]
        increment_ref[:, at : at + width] = projected[128:130]
        drop_ref[0:1, at : at + width] = jnp.sum(product[:64], axis=0, keepdims=True)
        drop_ref[1:2, at : at + width] = jnp.sum(product[64:], axis=0, keepdims=True)


def local(state_anom, obs_anom, innovations, obs_error, influence, taper_level, obs_count):
    sub_count = lax.axis_size("sub")
    regions = lax.axis_size("region")
    col_blocks, members, cells = state_anom.shape
    blocks = obs_anom.shape[0]
    assert (col_blocks, members, obs_anom.shape[2]) == (2, 64, 128)
    assert regions % 2 == 0 and sub_count in (4, 16, 64)
    vmem = pl.BlockSpec(memory_space=pltpu.VMEM)
    half = sub_count // 2
    wide, narrow = sum_rows(half, 8), sum_rows(half, 2)
    params = pltpu.CompilerParams(vmem_limit_bytes=VMEM_LIMIT)

    def sums(rows, dtype=jnp.bfloat16):
        return jax.ShapeDtypeStruct((rows, 128), dtype)

    place = pl.pallas_call(
        place_kernel,
        out_shape=jax.ShapeDtypeStruct((1, 128), jnp.int32),
        out_specs=vmem,
        compiler_params=pltpu.CompilerParams(vmem_limit_bytes=VMEM_LIMIT),
        cost_estimate=HEAD_COST,
    )()
    obs_count, place = lax.optimization_barrier((obs_count, place))
    terms, weights, far = pl.pallas_call(
        functools.partial(terms_kernel, sub_count, regions),
        out_shape=(
            jax.ShapeDtypeStruct((blocks, USED, 128), jnp.float32),
            jax.ShapeDtypeStruct((3 * sub_count, blocks, 128), jnp.float32),
            sums(wide),
        ),
        in_specs=[pl.BlockSpec(memory_space=pltpu.SMEM)] + [vmem] * 6,
        out_specs=(vmem,) * 3,
        scratch_shapes=[
            pltpu.VMEM((8, 128), jnp.float32),
            pltpu.VMEM((blocks, 128), jnp.float32),
            pltpu.VMEM((blocks, 128), jnp.float32),
        ],
        compiler_params=pltpu.CompilerParams(vmem_limit_bytes=VMEM_LIMIT),
        cost_estimate=pl.CostEstimate(flops=2 * blocks * 80 * 256 * 128, bytes_accessed=blocks * 64 * 128 * 2, transcendentals=0),
    )(obs_count, place, influence.T, taper_level.T, innovations, obs_error, obs_anom)
    state_anom, far = lax.optimization_barrier((state_anom, far))
    devices = [(r, s) for r in range(regions) for s in range(sub_count)]
    index = {device: i for i, device in enumerate(devices)}

    def moved(x, region_to, step=0):
        return lax.ppermute(x, AXES, [(index[r, s], index[region_to(r), s ^ step]) for r, s in devices])

    def sibling(r):
        return r ^ 1

    def across(r):
        return (r + 2 * (r % 2) - 1) % regions

    from_far = moved(far, across)
    near, far_later = pl.pallas_call(
        functools.partial(near_kernel, sub_count),
        out_shape=(sums(narrow), sums(wide)),
        in_specs=[vmem] * 2,
        out_specs=(vmem, vmem),
        compiler_params=params,
        cost_estimate=pl.CostEstimate(flops=blocks * wide * 256, bytes_accessed=blocks * USED * 512, transcendentals=0),
    )(terms, weights)
    from_near = moved(near, sibling)
    from_far_later = moved(far_later, lambda r: sibling(across(r)))
    here, beside, later = pl.pallas_call(
        functools.partial(rest_kernel, sub_count),
        out_shape=(sums(wide, jnp.float32), sums(wide + 8), sums(wide, jnp.float32)),
        in_specs=[vmem] * 2,
        out_specs=(vmem,) * 3,
        compiler_params=params,
        cost_estimate=pl.CostEstimate(flops=3 * blocks * wide * 256, bytes_accessed=blocks * USED * 512, transcendentals=0),
    )(terms, weights)
    sent = pl.pallas_call(
        functools.partial(join_kernel, half),
        out_shape=sums(wide),
        in_specs=[vmem] * 3,
        out_specs=vmem,
        scratch_shapes=[pltpu.VMEM((wide, 128), jnp.float32)],
        compiler_params=params,
        cost_estimate=pl.CostEstimate(flops=wide * 256, bytes_accessed=wide * 1024, transcendentals=0),
    )(from_near, here, from_far)
    got = moved(sent, sibling, 1)
    parts = (moved(beside, sibling), got, later, from_far_later)
    step, count = 2, half
    while step < sub_count:
        sent, kept = pl.pallas_call(
            functools.partial(fold_kernel, count),
            out_shape=(sums(sum_rows(count // 2, 8)), sums(sum_rows(count // 2, 2))),
            in_specs=[vmem] * len(parts),
            out_specs=(vmem, vmem),
            scratch_shapes=[pltpu.VMEM((sum_rows(count, 8), 128), jnp.float32)],
            compiler_params=params,
            cost_estimate=pl.CostEstimate(flops=count * 64 * 128, bytes_accessed=count * 64 * 1024, transcendentals=0),
        )(*parts)
        got = moved(sent, sibling, step)
        parts = (moved(kept, sibling), got)
        step, count = 2 * step, count // 2
    increment, variance_drop = pl.pallas_call(
        project_kernel,
        out_shape=(jax.ShapeDtypeStruct((2, cells), jnp.float32),) * 2,
        in_specs=[vmem] * 3,
        out_specs=(vmem, vmem),
        scratch_shapes=[pltpu.VMEM((sum_rows(1, 8), 128), jnp.float32)],
        compiler_params=pltpu.CompilerParams(vmem_limit_bytes=VMEM_LIMIT),
        cost_estimate=pl.CostEstimate(flops=2 * 144 * 128 * cells, bytes_accessed=col_blocks * 64 * cells * 2, transcendentals=0),
    )(*parts, state_anom.reshape(col_blocks * members, cells))
    return (increment, variance_drop)


def solution(mesh):
    return jax.shard_map(
        local,
        mesh=mesh,
        in_specs=(
            P(AXES, None, None),
            P(AXES, None, None),
            P(AXES, None),
            P(AXES, None),
            P(AXES, None),
            P(AXES, None),
            P("region"),
        ),
        out_specs=(P(AXES, None), P(AXES, None)),
        check_vma=False,
    )
```
